512 devices in a mesh: bead: 16 (over x_lo, z), dom: 32 (over x_hi, y, core).
Axes of the slice: x: 4 (x_hi: 2, x_lo: 2; x = x_hi * 2 + x_lo), y: 8, z: 8, core: 2. Of those that a mesh axis runs over, the one named last changes fastest.
Arguments:
- positions: float32 [32, 24, 128, 128], P('bead', None, 'dom'), may hold values from -6 to 6
- momenta: float32 [32, 24, 128, 128], P('bead', None, 'dom'), may hold values from -6 to 6
- offsets: int32 [27], replicated, may hold values from 0 to 26, each once
- harmonic: float32 [24, 648], replicated, may hold values from -0.25 to 0.25
- cubic: float32 [576, 648], replicated, may hold values from -0.046875 to 0.046875
Outputs:
- new_positions: float32 [32, 24, 128, 128], P('bead', None, 'dom')
- new_momenta: float32 [32, 24, 128, 128], P('bead', None, 'dom')
The draws below stay inside these ranges and needn't reach their ends.
Inputs may be any that keep to these rules, and one draw needn't show every extreme that they name: A permutation of the 27 offsets: each cell offset with components in -1, 0, 1 is named once.
All inputs are finite; a program needn't handle non-finite values.
Results may differ from the reference program's by a relative error of at most 0.00007.
Values sent between devices are 32-bit elements; how exact they have to be, the bound alone decides.
No kernel may reach another device: no remote copies, remote signals or barrier semaphores. Data moves between devices by JAX's collectives and lax.ppermute only.
A program may use at most 128 MiB of HBM per device.

```python
import jax
import jax.numpy as jnp
import numpy as np
from jax import lax

COMP = 24
BEADS = 32
NOFF = 27
CY = 8
CZ = 16
NX = 128


def block_levels(key, dims, cuts, low, top_value):
    def one(dim, blocks):
        heights = jax.random.uniform(jax.random.fold_in(jax.random.fold_in(key, 6), dim), (blocks,), jnp.float32, low / len(cuts), top_value / len(cuts))
        return jnp.repeat(jnp.exp(heights), dims[dim] // blocks).reshape((-1,) + (1,) * (len(dims) - dim - 1))

    gain = one(*cuts[0])
    for cut in cuts[1:]:
        gain = gain * one(*cut)
    return gain


def normal_values(own_key, extent, scale, limit, split=(), kind=jnp.bfloat16):
    values = jax.random.normal(own_key, extent, jnp.float32) * scale
    if len(split) > 0:
        values = block_levels(own_key, extent, split, -0.22, 0.18) * values
    return jnp.clip(values, min=-limit, max=limit).astype(kind)


def setup_inputs(seed: int = 0) -> dict:
    key_of = jax.random.split(jax.random.key(seed), 6)
    positions = normal_values(key_of[0], (BEADS, COMP, NX, CY * CZ), 1.0, 6.0, ((0, 16), (2, 32)), jnp.float32)
    momenta = normal_values(key_of[1], (BEADS, COMP, NX, CY * CZ), 1.0, 6.0, ((0, 16), (2, 32)), jnp.float32)
    offsets = jax.random.permutation(key_of[2], NOFF).astype(jnp.int32)
    harmonic = normal_values(key_of[3], (COMP, NOFF * COMP), (NOFF * COMP) ** -0.5, 0.25, (), jnp.float32)
    cubic = normal_values(key_of[4], (COMP * COMP, NOFF * COMP), (NOFF * COMP * COMP) ** -0.5, 0.046875, (), jnp.float32)
    return {"positions": positions, "momenta": momenta, "offsets": offsets, "harmonic": harmonic, "cubic": cubic}


time_step = 0.5
cycle_freq = 1.0

def mode_tables(count):
    rows = np.arange(count)[:, None] * 1.0
    cols = np.arange(count)[None, :]
    angle = 2.0 * np.pi * rows * cols / count
    table = np.where(cols == 0, 1.0 / np.sqrt(count) + 0.0 * angle, np.where(cols < count // 2, np.sqrt(2.0 / count) * np.cos(angle), np.where(cols == count // 2, np.cos(np.pi * rows) / np.sqrt(count), np.sqrt(2.0 / count) * np.sin(angle))))
    freq = 2.0 * cycle_freq * np.sin(np.pi * np.arange(count) / count)
    cosine = np.cos(freq * time_step)
    sine_over = np.where(freq > 0, np.sin(freq * time_step) / np.where(freq > 0, freq, 1.0), time_step)
    spring = freq * np.sin(freq * time_step)
    return (table, cosine, sine_over, spring)

def wrap_shift(field, step, axis):
    length = field.shape[axis]
    doubled = jnp.concatenate([field, field], axis)
    begin = jnp.remainder(step, length).astype(jnp.int32)
    return lax.dynamic_slice_in_dim(doubled, begin, length, axis)

def bead_force(field, offsets, harmonic, cubic):
    grid = field.reshape(COMP, NX, CY, CZ)
    parts = []
    for index in range(NOFF):
        code = offsets[index]
        moved = wrap_shift(grid, code // 9 - 1, 1)
        moved = wrap_shift(moved, code // 3 % 3 - 1, 2)
        moved = wrap_shift(moved, code % 3 - 1, 3)
        parts.append(moved.reshape(COMP, -1))
    stacked = jnp.concatenate(parts, 0)
    own = field.reshape(COMP, -1)
    linear = jnp.dot(harmonic, stacked, precision=lax.Precision.HIGHEST, preferred_element_type=jnp.float32)
    rows = jnp.dot(cubic, stacked, precision=lax.Precision.HIGHEST, preferred_element_type=jnp.float32)
    rows = rows.reshape(COMP, COMP, -1)
    anharm = lax.optimization_barrier(jnp.sum(rows * own[None, :, :], axis=1))
    return (-(linear + anharm)).reshape(field.shape)

def all_forces(field, offsets, harmonic, cubic):
    return lax.map(lambda one: bead_force(one, offsets, harmonic, cubic), field)

def reference(positions, momenta, offsets, harmonic, cubic):
    table, cosine, sine_over, spring = mode_tables(BEADS)
    table = jnp.asarray(table, jnp.float32)
    cosine = jnp.asarray(cosine, jnp.float32)[:, None, None, None]
    sine_over = jnp.asarray(sine_over, jnp.float32)[:, None, None, None]
    spring = jnp.asarray(spring, jnp.float32)[:, None, None, None]
    half = momenta + 0.5 * time_step * all_forces(positions, offsets, harmonic, cubic)
    mode_pos = jnp.einsum('bk,bcxy->kcxy', table, positions, precision=lax.Precision.HIGHEST)
    mode_mom = jnp.einsum('bk,bcxy->kcxy', table, half, precision=lax.Precision.HIGHEST)
    rot_pos = cosine * mode_pos + sine_over * mode_mom
    rot_mom = cosine * mode_mom - spring * mode_pos
    new_positions = jnp.einsum('bk,kcxy->bcxy', table, rot_pos, precision=lax.Precision.HIGHEST)
    middle = jnp.einsum('bk,kcxy->bcxy', table, rot_mom, precision=lax.Precision.HIGHEST)
    new_momenta = middle + 0.5 * time_step * all_forces(new_positions, offsets, harmonic, cubic)
    return (new_positions, new_momenta)
```

```python
import functools

import jax
import jax.numpy as jnp
import numpy as np
from jax import lax
from jax.experimental import pallas as pl
from jax.experimental.pallas import tpu as pltpu
from jax.sharding import PartitionSpec as P

BEADS = 32
COMP = 24
NOFF = 27
CZ = 16
CELLS = 128
OWN = 4
EXT = OWN + 2
BLOCK = 224
PLANE = 3 * BLOCK
DEPTH = 2048
ROWS = 608
TIME_STEP = 0.5
CYCLE_FREQ = 1.0
KICK = 0.5 * TIME_STEP

VMEM = pl.BlockSpec(memory_space=pltpu.VMEM)
SMEM = pl.BlockSpec(memory_space=pltpu.SMEM)
f32 = jnp.float32
bf16 = jnp.bfloat16


def propagator(groups):
    count = BEADS
    rows = np.arange(count)[:, None] * 1.0
    cols = np.arange(count)[None, :]
    angle = 2.0 * np.pi * rows * cols / count
    table = np.where(
        cols == 0,
        1.0 / np.sqrt(count) + 0.0 * angle,
        np.where(
            cols < count // 2,
            np.sqrt(2.0 / count) * np.cos(angle),
            np.where(
                cols == count // 2,
                np.cos(np.pi * rows) / np.sqrt(count),
                np.sqrt(2.0 / count) * np.sin(angle),
            ),
        ),
    )
    freq = 2.0 * CYCLE_FREQ * np.sin(np.pi * np.arange(count) / count)
    cosine = np.cos(freq * TIME_STEP)
    sine_over = np.where(
        freq > 0, np.sin(freq * TIME_STEP) / np.where(freq > 0, freq, 1.0), TIME_STEP
    )
    spring = freq * np.sin(freq * TIME_STEP)
    turn = (table * cosine) @ table.T
    drift = (table * sine_over) @ table.T
    pull = (table * spring) @ table.T
    whole = np.block([[turn, drift], [-pull, turn]])
    per = count // groups
    order = np.arange(2 * count).reshape(2, groups, per).transpose(0, 2, 1).reshape(-1)
    return whole[np.ix_(order, order)].astype(np.float32)


def put_neighbours(ns_ref, slot, bead, field):
    z = lax.broadcasted_iota(jnp.int32, field.shape, 1) % CZ
    up = jnp.where(z == CZ - 1, pltpu.roll(field, CZ - 1, 1), pltpu.roll(field, CELLS - 1, 1))
    down = jnp.where(z == 0, pltpu.roll(field, CELLS - CZ + 1, 1), pltpu.roll(field, 1, 1))
    along_z = [down, field, up]
    parts = [pltpu.roll(v, CZ, 1) for v in along_z]
    parts += along_z
    parts += [pltpu.roll(v, CELLS - CZ, 1) for v in along_z]
    parts.append(jnp.zeros((BLOCK - 9 * COMP, CELLS), f32))
    stack = jnp.concatenate(parts, 0)
    high = stack.astype(bf16)
    low = (stack - high.astype(f32)).astype(bf16)
    lanes = pl.ds(bead * CELLS, CELLS)
    ns_ref[pl.ds(slot * PLANE, BLOCK), lanes] = high
    ns_ref[pl.ds(slot * PLANE + BLOCK, BLOCK), lanes] = low
    ns_ref[pl.ds(slot * PLANE + 2 * BLOCK, BLOCK), lanes] = high


def force_of(w_ref, ns_ref, slot, own):
    rows = jnp.dot(w_ref[...], ns_ref[pl.ds(slot * PLANE, DEPTH), :], preferred_element_type=f32)
    higher = rows[: COMP * COMP].reshape(COMP, COMP, 2 * CELLS)
    anharm = jnp.sum(higher * own[None, :, :], axis=1)
    return -(rows[COMP * COMP : COMP * COMP + COMP] + anharm)


def own_plane(ref, bead, plane):
    return ref[pl.ds(bead * COMP * OWN + plane, COMP, stride=OWN), :]


def pack_kernel(pos_ref, mom_ref, left_ref, right_ref):
    for bead in range(2):
        for place, ref, first, last in (
            (0, pos_ref, 0, 2),
            (1, pos_ref, 1, 3),
            (2, mom_ref, 0, 3),
        ):
            rows = pl.ds((place * 2 + bead) * COMP, COMP)
            left_ref[rows, :] = own_plane(ref, bead, first)
            right_ref[rows, :] = own_plane(ref, bead, last)


def inner_kernel(off_ref, harm_ref, cub_ref, pos_ref, mom_ref, w_ref, half_ref, hpad, hturn, wt, cat, ns):
    hpad[...] = jnp.zeros_like(hpad)
    hpad[64 : 64 + COMP, 0 : NOFF * COMP] = harm_ref[...]
    for tile in range(6):
        hturn[tile * 128 : (tile + 1) * 128, :] = hpad[:, tile * 128 : (tile + 1) * 128].T
    for dx in range(3):
        wt[dx * BLOCK + 9 * COMP : (dx + 1) * BLOCK, :] = jnp.zeros((8, 640), f32)
    for o in range(NOFF):
        code = off_ref[o]
        rows = pl.ds(pl.multiple_of(code * COMP + (code // 9) * 8, 8), COMP)
        wt[rows, 512:640] = hturn[o * COMP : (o + 1) * COMP, :]
        wt[rows, 0 : COMP * COMP] = cub_ref[o * COMP : (o + 1) * COMP, :]
    for dx in range(3):
        block = wt[dx * BLOCK : (dx + 1) * BLOCK, :]
        high = block.astype(bf16)
        low = (block - high.astype(f32)).astype(bf16)
        cat[dx * PLANE : dx * PLANE + BLOCK, :] = high
        cat[dx * PLANE + BLOCK : dx * PLANE + 2 * BLOCK, :] = high
        cat[dx * PLANE + 2 * BLOCK : (dx + 1) * PLANE, :] = low
    cat[3 * PLANE : DEPTH, :] = jnp.zeros((DEPTH - 3 * PLANE, 640), bf16)
    for m in range(5):
        size = min(128, ROWS - m * 128)
        for k in range(DEPTH // 128):
            turned = cat[k * 128 : (k + 1) * 128, m * 128 : (m + 1) * 128].T
            w_ref[m * 128 : m * 128 + size, k * 128 : (k + 1) * 128] = turned[:size]
    ns[OWN * PLANE : OWN * PLANE + 32, :] = jnp.zeros((32, 2 * CELLS), bf16)
    for plane in range(OWN):
        for bead in range(2):
            put_neighbours(ns, plane, bead, own_plane(pos_ref, bead, plane))
    for plane in (1, 2):
        own = jnp.concatenate([own_plane(pos_ref, bead, plane) for bead in range(2)], 1)
        mom = jnp.concatenate([own_plane(mom_ref, bead, plane) for bead in range(2)], 1)
        half_ref[(plane - 1) * COMP : plane * COMP, :] = mom + KICK * force_of(w_ref, ns, plane - 1, own)


def outer_kernel(w_ref, pos_ref, mom_ref, half_ref, left_ref, right_ref, send_ref, ns):
    def block(ref, place, bead):
        return ref[(place * 2 + bead) * COMP : (place * 2 + bead + 1) * COMP, :]

    def position(plane, bead):
        if plane < 0:
            return block(left_ref, plane + 2, bead)
        if plane >= OWN:
            return block(right_ref, plane - OWN, bead)
        return own_plane(pos_ref, bead, plane)

    def momentum(plane, bead):
        if plane < 0:
            return block(left_ref, 2, bead)
        if plane >= OWN:
            return block(right_ref, 2, bead)
        return own_plane(mom_ref, bead, plane)

    def store(plane, kind, bead, value):
        send_ref[pl.ds((plane + 1) * COMP * 4 + kind * 2 + bead, COMP, stride=4), :] = value

    ns[8 * PLANE : 8 * PLANE + 32, :] = jnp.zeros((32, 2 * CELLS), bf16)
    for plane in range(-2, OWN + 2):
        for bead in range(2):
            put_neighbours(ns, plane + 2, bead, position(plane, bead))
    for plane in range(-1, OWN + 1):
        for bead in range(2):
            store(plane, 0, bead, position(plane, bead))
    for plane in (1, 2):
        for bead in range(2):
            store(plane, 1, bead, half_ref[(plane - 1) * COMP : plane * COMP, bead * CELLS : (bead + 1) * CELLS])
    for plane in (-1, 0, OWN - 1, OWN):
        own = jnp.concatenate([position(plane, bead) for bead in range(2)], 1)
        force = force_of(w_ref, ns, plane + 1, own)
        for bead in range(2):
            half = momentum(plane, bead) + KICK * force[:, bead * CELLS : (bead + 1) * CELLS]
            store(plane, 1, bead, half)


def bead_kernel(groups, rows, map_ref, in_ref, out_ref):
    columns = []
    for r in range(rows):
        columns.append(
            jnp.concatenate([in_ref[pl.ds(r * 4 + q, groups, stride=rows * 4), :] for q in range(4)], 0)
        )
    moved = jnp.dot(
        map_ref[...],
        jnp.concatenate(columns, 1),
        precision=lax.Precision.HIGHEST,
        preferred_element_type=f32,
    )
    for r in range(rows):
        for q in range(4):
            out_ref[pl.ds(r * 4 + q, groups, stride=rows * 4), :] = moved[
                q * groups : (q + 1) * groups, r * CELLS : (r + 1) * CELLS
            ]


def last_kernel(w_ref, in_ref, pos_ref, mom_ref, ns):
    def value(plane, kind, bead):
        return in_ref[pl.ds(plane * COMP * 4 + kind * 2 + bead, COMP, stride=4), :]

    ns[EXT * PLANE : EXT * PLANE + 32, :] = jnp.zeros((32, 2 * CELLS), bf16)
    for plane in range(EXT):
        for bead in range(2):
            field = value(plane, 0, bead)
            put_neighbours(ns, plane, bead, field)
            if 1 <= plane <= OWN:
                pos_ref[pl.ds(bead * COMP * OWN + plane - 1, COMP, stride=OWN), :] = field
    for plane in range(1, OWN + 1):
        own = jnp.concatenate([value(plane, 0, bead) for bead in range(2)], 1)
        force = force_of(w_ref, ns, plane - 1, own)
        for bead in range(2):
            mom_ref[pl.ds(bead * COMP * OWN + plane - 1, COMP, stride=OWN), :] = (
                value(plane, 1, bead) + KICK * force[:, bead * CELLS : (bead + 1) * CELLS]
            )


def call(kernel, name, ins, outs, scratch, flops, *args):
    size = sum(int(np.prod(a.shape)) * a.dtype.itemsize for a in (*args, *outs))
    return pl.pallas_call(
        kernel,
        name=name,
        in_specs=ins,
        out_specs=[VMEM] * len(outs),
        out_shape=list(outs),
        scratch_shapes=scratch,
        compiler_params=pltpu.CompilerParams(vmem_limit_bytes=24 * 1024 * 1024),
        cost_estimate=pl.CostEstimate(flops=flops, bytes_accessed=size, transcendentals=0),
    )(*args)


def neighbours(planes):
    return pltpu.VMEM((planes * PLANE + 32, 2 * CELLS), bf16)


def body(positions, momenta, offsets, harmonic, cubic):
    shape = jax.ShapeDtypeStruct
    per_plane = 2 * ROWS * DEPTH * 2 * CELLS
    groups = lax.axis_size("bead")
    doms = lax.axis_size("dom")
    pos = positions.reshape(2 * COMP * OWN, CELLS)
    mom = momenta.reshape(2 * COMP * OWN, CELLS)
    planes = shape((6 * COMP, CELLS), f32)
    to_left, to_right = call(pack_kernel, "pack", [VMEM] * 2, [planes] * 2, [], 0, pos, mom)
    from_left = lax.ppermute(to_right, "dom", [(i, (i + 1) % doms) for i in range(doms)])
    from_right = lax.ppermute(to_left, "dom", [((i + 1) % doms, i) for i in range(doms)])
    weights, half = call(
        inner_kernel,
        "inner",
        [SMEM] + [VMEM] * 4,
        [shape((ROWS, DEPTH), bf16), shape((2 * COMP, 2 * CELLS), f32)],
        [
            pltpu.VMEM((128, 768), f32),
            pltpu.VMEM((768, 128), f32),
            pltpu.VMEM((PLANE, 640), f32),
            pltpu.VMEM((DEPTH, 640), bf16),
            neighbours(OWN),
        ],
        2 * per_plane,
        offsets,
        harmonic,
        cubic.T,
        pos,
        mom,
    )
    rows = EXT * COMP // groups
    exchanged = shape((groups * rows * 4, CELLS), f32)
    (send,) = call(
        outer_kernel, "outer", [VMEM] * 6, [exchanged], [neighbours(8)], 4 * per_plane,
        weights, pos, mom, half, from_left, from_right,
    )

    def swap(x):
        x = lax.all_to_all(x.reshape(groups, rows, 4, CELLS), "bead", 0, 0, tiled=True)
        return x.reshape(groups * rows * 4, CELLS)

    (back,) = call(
        functools.partial(bead_kernel, groups, rows), "beads", [VMEM] * 2, [exchanged], [],
        2 * 64 * 64 * 6 * rows * CELLS, jnp.asarray(propagator(groups)), swap(send),
    )
    own = shape((2 * COMP * OWN, CELLS), f32)
    new_pos, new_mom = call(
        last_kernel, "last", [VMEM] * 2, [own] * 2, [neighbours(EXT)], 4 * per_plane, weights, swap(back)
    )
    return new_pos.reshape(positions.shape), new_mom.reshape(momenta.shape)


def solution(mesh):
    return jax.shard_map(
        body,
        mesh=mesh,
        in_specs=(P("bead", None, "dom", None), P("bead", None, "dom", None), P(), P(), P()),
        out_specs=(P("bead", None, "dom", None), P("bead", None, "dom", None)),
        check_vma=False,
    )
```

```python
import jax
import jax.numpy as jnp
import numpy as np
from jax import lax
from jax.experimental import pallas as pl
from jax.experimental.pallas import tpu as pltpu
from jax.sharding import PartitionSpec as P

BEADS = 32
COMP = 24
NOFF = 27
CZ = 16
CELLS = 128
OWN = 4
EXT = OWN + 2
BLOCK = 224
PLANE = 3 * BLOCK
DEPTH = 2048
ROWS = 608
TIME_STEP = 0.5
CYCLE_FREQ = 1.0
KICK = 0.5 * TIME_STEP

EARLY = 10_000_000_000
GROUP = 16
SMEM = pl.BlockSpec(memory_space=pltpu.SMEM)
VMEM = pl.BlockSpec(memory_space=pltpu.VMEM)
f32 = jnp.float32
bf16 = jnp.bfloat16


def propagator(groups):
    count = BEADS
    rows = np.arange(count)[:, None] * 1.0
    cols = np.arange(count)[None, :]
    angle = 2.0 * np.pi * rows * cols / count
    table = np.where(
        cols == 0,
        1.0 / np.sqrt(count) + 0.0 * angle,
        np.where(
            cols < count // 2,
            np.sqrt(2.0 / count) * np.cos(angle),
            np.where(
                cols == count // 2,
                np.cos(np.pi * rows) / np.sqrt(count),
                np.sqrt(2.0 / count) * np.sin(angle),
            ),
        ),
    )
    freq = 2.0 * CYCLE_FREQ * np.sin(np.pi * np.arange(count) / count)
    cosine = np.cos(freq * TIME_STEP)
    sine_over = np.where(
        freq > 0, np.sin(freq * TIME_STEP) / np.where(freq > 0, freq, 1.0), TIME_STEP
    )
    spring = freq * np.sin(freq * TIME_STEP)
    turn = (table * cosine) @ table.T
    drift = (table * sine_over) @ table.T
    pull = (table * spring) @ table.T
    whole = np.block([[turn, drift], [-pull, turn]])
    per = count // groups
    order = np.arange(2 * count).reshape(2, groups, per).transpose(0, 2, 1).reshape(-1)
    return whole[np.ix_(order, order)].astype(np.float32)


def put_neighbours(ns_ref, slot, bead, field):
    z = lax.broadcasted_iota(jnp.int32, field.shape, 1) % CZ
    up = jnp.where(z == CZ - 1, pltpu.roll(field, CZ - 1, 1), pltpu.roll(field, CELLS - 1, 1))
    down = jnp.where(z == 0, pltpu.roll(field, CELLS - CZ + 1, 1), pltpu.roll(field, 1, 1))
    along_z = [down, field, up]
    parts = [pltpu.roll(v, CZ, 1) for v in along_z]
    parts += along_z
    parts += [pltpu.roll(v, CELLS - CZ, 1) for v in along_z]
    parts.append(jnp.zeros((BLOCK - 9 * COMP, CELLS), f32))
    stack = jnp.concatenate(parts, 0)
    high = stack.astype(bf16)
    low = (stack - high.astype(f32)).astype(bf16)
    lanes = pl.ds(bead * CELLS, CELLS)
    ns_ref[pl.ds(slot * PLANE, BLOCK), lanes] = high
    ns_ref[pl.ds(slot * PLANE + BLOCK, BLOCK), lanes] = low
    ns_ref[pl.ds(slot * PLANE + 2 * BLOCK, BLOCK), lanes] = high


def force_of(w_ref, ns_ref, slot, own):
    rows = jnp.dot(w_ref[...], ns_ref[pl.ds(slot * PLANE, DEPTH), :], preferred_element_type=f32)
    higher = rows[: COMP * COMP].reshape(COMP, COMP, 2 * CELLS)
    anharm = jnp.sum(higher * own[None, :, :], axis=1)
    return -(rows[COMP * COMP : COMP * COMP + COMP] + anharm)


def halves(core, here, there):
    return jnp.where(core == 0, here, there)


def own_plane(ref, bead, plane):
    return ref[pl.ds(bead * COMP * OWN + plane, COMP, stride=OWN), :]


def block(ref, place, bead):
    return ref[(place * 2 + bead) * COMP : (place * 2 + bead + 1) * COMP, :]


def planes_kernel(ref, planes_ref):
    for plane in range(OWN):
        for bead in range(2):
            planes_ref[pl.ds((plane * 2 + bead) * COMP, COMP), :] = own_plane(ref, bead, plane)


def pack_kernel(pos_ref, raw_ref, far_ref, near_ref, mom_ref):
    core = lax.axis_index("dom") % 2
    planes_kernel(raw_ref, mom_ref)
    for bead in range(2):
        pos = [block(pos_ref, plane, bead) for plane in range(OWN)]
        first, last = block(mom_ref, 0, bead), block(mom_ref, OWN - 1, bead)
        for place, left, right in ((0, pos[0], pos[2]), (1, pos[1], pos[3]), (2, first, last)):
            rows = pl.ds((place * 2 + bead) * COMP, COMP)
            far_ref[rows, :] = halves(core, left, right)
            near_ref[rows, :] = halves(core, right, left)


def inner_kernel(off_ref, harm_ref, cub_ref, pos_ref, mom_ref, w_ref, half_ref, hpad, hturn, wt, cat, ns):
    ns[OWN * PLANE : OWN * PLANE + 32, :] = jnp.zeros((32, 2 * CELLS), bf16)
    for plane in range(OWN):
        for bead in range(2):
            put_neighbours(ns, plane, bead, block(pos_ref, plane, bead))
    hpad[...] = jnp.zeros_like(hpad)
    hpad[64 : 64 + COMP, 0 : NOFF * COMP] = harm_ref[...]
    for tile in range(6):
        hturn[tile * 128 : (tile + 1) * 128, :] = hpad[:, tile * 128 : (tile + 1) * 128].T
    for dx in range(3):
        wt[dx * BLOCK + 9 * COMP : (dx + 1) * BLOCK, :] = jnp.zeros((8, 640), f32)
    for o in range(NOFF):
        code = off_ref[o]
        rows = pl.ds(pl.multiple_of(code * COMP + (code // 9) * 8, 8), COMP)
        wt[rows, 512:640] = hturn[o * COMP : (o + 1) * COMP, :]
        wt[rows, 0 : COMP * COMP] = cub_ref[o * COMP : (o + 1) * COMP, :]
    for dx in range(3):
        rows = wt[dx * BLOCK : (dx + 1) * BLOCK, :]
        high = rows.astype(bf16)
        low = (rows - high.astype(f32)).astype(bf16)
        cat[dx * PLANE : dx * PLANE + BLOCK, :] = high
        cat[dx * PLANE + BLOCK : dx * PLANE + 2 * BLOCK, :] = high
        cat[dx * PLANE + 2 * BLOCK : (dx + 1) * PLANE, :] = low
    cat[3 * PLANE : DEPTH, :] = jnp.zeros((DEPTH - 3 * PLANE, 640), bf16)
    for m in range(5):
        size = min(128, ROWS - m * 128)
        for k in range(DEPTH // 128):
            turned = cat[k * 128 : (k + 1) * 128, m * 128 : (m + 1) * 128].T
            w_ref[m * 128 : m * 128 + size, k * 128 : (k + 1) * 128] = turned[:size]
    for plane in (1, 2):
        own = jnp.concatenate([block(pos_ref, plane, bead) for bead in range(2)], 1)
        mom = jnp.concatenate([block(mom_ref, plane, bead) for bead in range(2)], 1)
        half_ref[(plane - 1) * COMP : plane * COMP, :] = mom + KICK * force_of(w_ref, ns, plane - 1, own)


def place_of(plane):
    return (0, plane) if plane < 3 else (1, EXT - 1 - plane)


def outer_kernel(w_ref, pos_ref, mom_ref, half_ref, far_ref, near_ref, send_ref, ns):
    core = lax.axis_index("dom") % 2
    left = [[halves(core, block(far_ref, i, bead), block(near_ref, i, bead)) for bead in range(2)] for i in range(3)]
    right = [[halves(core, block(near_ref, i, bead), block(far_ref, i, bead)) for bead in range(2)] for i in range(3)]

    def position(plane, bead):
        if plane < 0:
            return left[plane + 2][bead]
        if plane >= OWN:
            return right[plane - OWN][bead]
        return block(pos_ref, plane, bead)

    def momentum(plane, bead):
        if plane < 0:
            return left[2][bead]
        if plane >= OWN:
            return right[2][bead]
        return block(mom_ref, plane, bead)

    def store(plane, kind, bead, value):
        half, step = place_of(plane + 1)
        send_ref[pl.ds(half * 288 + step * 4 + kind * 2 + bead, COMP, stride=12), :] = value

    ns[8 * PLANE : 8 * PLANE + 32, :] = jnp.zeros((32, 2 * CELLS), bf16)
    for plane in range(-2, OWN + 2):
        for bead in range(2):
            put_neighbours(ns, plane + 2, bead, position(plane, bead))
    for plane in range(-1, OWN + 1):
        for bead in range(2):
            store(plane, 0, bead, position(plane, bead))
    for plane in (1, 2):
        for bead in range(2):
            store(plane, 1, bead, half_ref[(plane - 1) * COMP : plane * COMP, bead * CELLS : (bead + 1) * CELLS])
    for plane in (-1, 0, OWN - 1, OWN):
        own = jnp.concatenate([position(plane, bead) for bead in range(2)], 1)
        force = force_of(w_ref, ns, plane + 1, own)
        for bead in range(2):
            half = momentum(plane, bead) + KICK * force[:, bead * CELLS : (bead + 1) * CELLS]
            store(plane, 1, bead, half)


def bead_kernel(map_ref, in_ref, out_ref):
    columns = []
    for r in range(9):
        columns.append(jnp.concatenate([in_ref[pl.ds(r * 4 + q, GROUP, stride=36), :] for q in range(4)], 0))
    moved = jnp.dot(
        map_ref[...],
        jnp.concatenate(columns, 1),
        precision=lax.Precision.HIGHEST,
        preferred_element_type=f32,
    )
    for r in range(9):
        line, step = r // 3, r % 3
        for q in range(4):
            row = step * 2 + q if q < 2 else 6 + (step - 1) * 2 + q - 2
            if q < 2 or step > 0:
                out_ref[pl.ds(line * 10 + row, GROUP, stride=30), :] = moved[
                    q * GROUP : (q + 1) * GROUP, r * CELLS : (r + 1) * CELLS
                ]


def last_kernel(w_ref, in_ref, pos_ref, mom_ref, ns):
    def value(plane, kind, bead):
        half, step = place_of(plane)
        row = step * 2 + bead if kind == 0 else 6 + (step - 1) * 2 + bead
        return in_ref[pl.ds(half * 240 + row, COMP, stride=10), :]

    ns[EXT * PLANE : EXT * PLANE + 32, :] = jnp.zeros((32, 2 * CELLS), bf16)
    for plane in range(EXT):
        for bead in range(2):
            field = value(plane, 0, bead)
            put_neighbours(ns, plane, bead, field)
            if 1 <= plane <= OWN:
                pos_ref[pl.ds(bead * COMP * OWN + plane - 1, COMP, stride=OWN), :] = field
    for plane in range(1, OWN + 1):
        own = jnp.concatenate([value(plane, 0, bead) for bead in range(2)], 1)
        force = force_of(w_ref, ns, plane - 1, own)
        for bead in range(2):
            mom_ref[pl.ds(bead * COMP * OWN + plane - 1, COMP, stride=OWN), :] = (
                value(plane, 1, bead) + KICK * force[:, bead * CELLS : (bead + 1) * CELLS]
            )


def call(kernel, name, ins, outs, scratch, flops, *args):
    size = sum(int(np.prod(a.shape)) * a.dtype.itemsize for a in (*args, *outs))
    return pl.pallas_call(
        kernel,
        name=name,
        in_specs=ins,
        out_specs=[VMEM] * len(outs),
        out_shape=list(outs),
        scratch_shapes=scratch,
        compiler_params=pltpu.CompilerParams(vmem_limit_bytes=24 * 1024 * 1024),
        cost_estimate=pl.CostEstimate(flops=flops, bytes_accessed=size, transcendentals=0),
    )(*args)


def neighbours(planes):
    return pltpu.VMEM((planes * PLANE + 32, 2 * CELLS), bf16)


def body(positions, momenta, offsets, harmonic, cubic):
    shape = jax.ShapeDtypeStruct
    per_plane = 2 * ROWS * DEPTH * 2 * CELLS
    doms = lax.axis_size("dom")
    pos = positions.reshape(2 * COMP * OWN, CELLS)
    mom = momenta.reshape(2 * COMP * OWN, CELLS)
    own = shape((2 * COMP * OWN, CELLS), f32)
    halo = shape((6 * COMP, CELLS), f32)
    (pos,) = call(planes_kernel, "planes", [VMEM], [own], [], EARLY, pos)
    far, near, mom = call(pack_kernel, "pack", [VMEM] * 2, [halo, halo, own], [], EARLY, pos, mom)
    between = [(i, (i + 1) % doms) for i in range(1, doms, 2)]
    far = lax.ppermute(far, "dom", between + [(j, i) for i, j in between])
    near = lax.ppermute(near, "dom", [(i, i ^ 1) for i in range(doms)])
    weights, half = call(
        inner_kernel,
        "inner",
        [SMEM] + [VMEM] * 4,
        [shape((ROWS, DEPTH), bf16), shape((2 * COMP, 2 * CELLS), f32)],
        [
            pltpu.VMEM((128, 768), f32),
            pltpu.VMEM((768, 128), f32),
            pltpu.VMEM((PLANE, 640), f32),
            pltpu.VMEM((DEPTH, 640), bf16),
            neighbours(OWN),
        ],
        2 * per_plane,
        offsets,
        harmonic,
        cubic.T,
        pos,
        mom,
    )
    (send,) = call(
        outer_kernel, "outer", [VMEM] * 6, [shape((GROUP * 36, CELLS), f32)], [neighbours(8)], 4 * per_plane,
        weights, pos, mom, half, far, near,
    )
    got = lax.all_to_all(send.reshape(GROUP, 9, 4, CELLS), "bead", 0, 0, tiled=True)
    (back,) = call(
        bead_kernel, "beads", [VMEM] * 2, [shape((GROUP * 30, CELLS), f32)], [], 2 * 64 * 64 * 9 * CELLS,
        jnp.asarray(propagator(GROUP)), got.reshape(GROUP * 36, CELLS),
    )
    got = lax.all_to_all(back.reshape(GROUP, 15, 2, CELLS), "bead", 0, 0, tiled=True)
    new_pos, new_mom = call(
        last_kernel, "last", [VMEM] * 2, [own] * 2, [neighbours(EXT)], 4 * per_plane,
        weights, got.reshape(GROUP * 30, CELLS),
    )
    return new_pos.reshape(positions.shape), new_mom.reshape(momenta.shape)


def solution(mesh):
    return jax.shard_map(
        body,
        mesh=mesh,
        in_specs=(P("bead", None, "dom", None), P("bead", None, "dom", None), P(), P(), P()),
        out_specs=(P("bead", None, "dom", None), P("bead", None, "dom", None)),
        check_vma=False,
    )
```

```python
import jax
import jax.numpy as jnp
import numpy as np
from jax import lax
from jax.experimental import pallas as pl
from jax.experimental.pallas import tpu as pltpu
from jax.sharding import PartitionSpec as P

BEADS = 32
COMP = 24
NOFF = 27
CZ = 16
CELLS = 128
OWN = 4
EXT = OWN + 2
BLOCK = 224
PLANE = 3 * BLOCK
DEPTH = 2048
ROWS = 608
TIME_STEP = 0.5
CYCLE_FREQ = 1.0
KICK = 0.5 * TIME_STEP

EARLY = 10_000_000_000
GROUP = 16
HBM = pl.BlockSpec(memory_space=pltpu.HBM)
SMEM = pl.BlockSpec(memory_space=pltpu.SMEM)
VMEM = pl.BlockSpec(memory_space=pltpu.VMEM)
f32 = jnp.float32
bf16 = jnp.bfloat16


def propagator(groups):
    count = BEADS
    rows = np.arange(count)[:, None] * 1.0
    cols = np.arange(count)[None, :]
    angle = 2.0 * np.pi * rows * cols / count
    table = np.where(
        cols == 0,
        1.0 / np.sqrt(count) + 0.0 * angle,
        np.where(
            cols < count // 2,
            np.sqrt(2.0 / count) * np.cos(angle),
            np.where(
                cols == count // 2,
                np.cos(np.pi * rows) / np.sqrt(count),
                np.sqrt(2.0 / count) * np.sin(angle),
            ),
        ),
    )
    freq = 2.0 * CYCLE_FREQ * np.sin(np.pi * np.arange(count) / count)
    cosine = np.cos(freq * TIME_STEP)
    sine_over = np.where(
        freq > 0, np.sin(freq * TIME_STEP) / np.where(freq > 0, freq, 1.0), TIME_STEP
    )
    spring = freq * np.sin(freq * TIME_STEP)
    turn = (table * cosine) @ table.T
    drift = (table * sine_over) @ table.T
    pull = (table * spring) @ table.T
    whole = np.block([[turn, drift], [-pull, turn]])
    per = count // groups
    order = np.arange(2 * count).reshape(2, groups, per).transpose(0, 2, 1).reshape(-1)
    return whole[np.ix_(order, order)].astype(np.float32)


def put_neighbours(ns_ref, row, bead, field):
    z = lax.broadcasted_iota(jnp.int32, field.shape, 1) % CZ
    up = jnp.where(z == CZ - 1, pltpu.roll(field, CZ - 1, 1), pltpu.roll(field, CELLS - 1, 1))
    down = jnp.where(z == 0, pltpu.roll(field, CELLS - CZ + 1, 1), pltpu.roll(field, 1, 1))
    along_z = [down, field, up]
    parts = [pltpu.roll(v, CZ, 1) for v in along_z]
    parts += along_z
    parts += [pltpu.roll(v, CELLS - CZ, 1) for v in along_z]
    parts.append(jnp.zeros((BLOCK - 9 * COMP, CELLS), f32))
    stack = jnp.concatenate(parts, 0)
    high = stack.astype(bf16)
    low = (stack - high.astype(f32)).astype(bf16)
    lanes = pl.ds(bead * CELLS, CELLS)
    ns_ref[pl.ds(row, BLOCK), lanes] = high
    ns_ref[pl.ds(row + BLOCK, BLOCK), lanes] = low
    ns_ref[pl.ds(row + 2 * BLOCK, BLOCK), lanes] = high


def product(w_ref, first, depth, ns_ref, row):
    return jnp.dot(
        w_ref[:, pl.ds(first, depth)], ns_ref[pl.ds(row, depth), :], preferred_element_type=f32
    )


def force_from(rows, own):
    higher = rows[: COMP * COMP].reshape(COMP, COMP, 2 * CELLS)
    anharm = jnp.sum(higher * own[None, :, :], axis=1)
    return -(rows[COMP * COMP : COMP * COMP + COMP] + anharm)


def halves(core, here, there):
    return jnp.where(core == 0, here, there)


def own_plane(ref, bead, plane):
    return ref[pl.ds(bead * COMP * OWN + plane, COMP, stride=OWN), :]


def block(ref, place, bead):
    return ref[(place * 2 + bead) * COMP : (place * 2 + bead + 1) * COMP, :]


def pair(ref, place):
    return jnp.concatenate([block(ref, place, bead) for bead in range(2)], 1)


def clear(ref, row, count):
    ref[row : row + count, :] = jnp.zeros((count, ref.shape[1]), ref.dtype)


def tick_kernel(out_ref):
    clear(out_ref, 0, 8)


def planes_kernel(ref, planes_ref):
    for plane in range(OWN):
        for bead in range(2):
            planes_ref[pl.ds((plane * 2 + bead) * COMP, COMP), :] = own_plane(ref, bead, plane)


def pack_kernel(blank_ref, raw_pos_ref, raw_mom_ref, far_ref, near_ref, pos_ref, mom_ref):
    core = lax.axis_index("dom") % 2
    planes_kernel(raw_pos_ref, pos_ref)
    planes_kernel(raw_mom_ref, mom_ref)
    for bead in range(2):
        pos = [own_plane(raw_pos_ref, bead, plane) for plane in range(OWN)]
        first, last = (own_plane(raw_mom_ref, bead, plane) for plane in (0, OWN - 1))
        for place, left, right in ((0, pos[0], pos[2]), (1, pos[1], pos[3]), (2, first, last)):
            rows = pl.ds((place * 2 + bead) * COMP, COMP)
            far_ref[rows, :] = halves(core, left, right)
            near_ref[rows, :] = halves(core, right, left)


def inner_kernel(
    off_ref, harm_ref, cub_ref, pos_ref, mom_ref, w_ref, half_ref, side_ref, before_ref, after_ref, hpad, hturn, wt, cat, ns
):
    clear(ns, 0, 64)
    clear(ns, 64 + OWN * PLANE, 96)
    for plane in range(OWN):
        for bead in range(2):
            put_neighbours(ns, 64 + plane * PLANE, bead, block(pos_ref, plane, bead))
    hpad[...] = jnp.zeros_like(hpad)
    hpad[64 : 64 + COMP, 0 : NOFF * COMP] = harm_ref[...]
    for tile in range(6):
        hturn[tile * 128 : (tile + 1) * 128, :] = hpad[:, tile * 128 : (tile + 1) * 128].T
    for dx in range(3):
        wt[dx * BLOCK + 9 * COMP : (dx + 1) * BLOCK, :] = jnp.zeros((8, 640), f32)
    for o in range(NOFF):
        code = off_ref[o]
        rows = pl.ds(pl.multiple_of(code * COMP + (code // 9) * 8, 8), COMP)
        wt[rows, 512:640] = hturn[o * COMP : (o + 1) * COMP, :]
        wt[rows, 0 : COMP * COMP] = cub_ref[o * COMP : (o + 1) * COMP, :]
    for dx in range(3):
        rows = wt[dx * BLOCK : (dx + 1) * BLOCK, :]
        high = rows.astype(bf16)
        low = (rows - high.astype(f32)).astype(bf16)
        cat[dx * PLANE : dx * PLANE + BLOCK, :] = high
        cat[dx * PLANE + BLOCK : dx * PLANE + 2 * BLOCK, :] = high
        cat[dx * PLANE + 2 * BLOCK : (dx + 1) * PLANE, :] = low
    cat[3 * PLANE : DEPTH, :] = jnp.zeros((DEPTH - 3 * PLANE, 640), bf16)
    for m in range(5):
        size = min(128, ROWS - m * 128)
        for k in range(DEPTH // 128):
            turned = cat[k * 128 : (k + 1) * 128, m * 128 : (m + 1) * 128].T
            w_ref[m * 128 : m * 128 + size, k * 128 : (k + 1) * 128] = turned[:size]
    for plane in (1, 2):
        force = force_from(product(w_ref, 0, DEPTH, ns, 64 + (plane - 1) * PLANE), pair(pos_ref, plane))
        half_ref[(plane - 1) * COMP : plane * COMP, :] = pair(mom_ref, plane) + KICK * force
    side_ref[0:COMP, :] = force_from(product(w_ref, 640, 1408, ns, 32), pair(pos_ref, 0))
    side_ref[COMP:, :] = force_from(product(w_ref, 0, 1408, ns, 64 + 2 * PLANE), pair(pos_ref, OWN - 1))
    before_ref[...] = product(w_ref, 1280, 768, ns, 0)
    after_ref[...] = product(w_ref, 0, 768, ns, 64 + 3 * PLANE)


def place_of(plane):
    return (0, plane) if plane < 3 else (1, EXT - 1 - plane)


def outer_kernel(
    w_ref, pos_ref, mom_ref, half_ref, side_ref, before_ref, after_ref, far_ref, near_ref, send_ref, lower, upper
):
    core = lax.axis_index("dom") % 2
    left = [[halves(core, block(far_ref, i, bead), block(near_ref, i, bead)) for bead in range(2)] for i in range(3)]
    right = [[halves(core, block(near_ref, i, bead), block(far_ref, i, bead)) for bead in range(2)] for i in range(3)]

    def position(plane, bead):
        if plane < 0:
            return left[plane + 2][bead]
        if plane >= OWN:
            return right[plane - OWN][bead]
        return block(pos_ref, plane, bead)

    def momentum(plane, bead):
        if plane < 0:
            return left[2][bead]
        if plane >= OWN:
            return right[2][bead]
        return block(mom_ref, plane, bead)

    def store(plane, kind, bead, value):
        half, step = place_of(plane + 1)
        send_ref[pl.ds(half * 288 + step * 4 + kind * 2 + bead, COMP, stride=12), :] = value

    clear(lower, 2 * PLANE, 96)
    clear(upper, 0, 64)
    clear(upper, 64 + 2 * PLANE, 32)
    for i in range(2):
        for bead in range(2):
            put_neighbours(lower, i * PLANE, bead, left[i][bead])
            put_neighbours(upper, 64 + i * PLANE, bead, right[i][bead])
    for plane in range(-1, OWN + 1):
        for bead in range(2):
            store(plane, 0, bead, position(plane, bead))
    for plane in (1, 2):
        for bead in range(2):
            store(plane, 1, bead, half_ref[(plane - 1) * COMP : plane * COMP, bead * CELLS : (bead + 1) * CELLS])
    for plane in (-1, 0, OWN - 1, OWN):
        own = jnp.concatenate([position(plane, bead) for bead in range(2)], 1)
        if plane == -1:
            force = force_from(before_ref[...] + product(w_ref, 0, 1408, lower, 0), own)
        elif plane == 0:
            force = side_ref[0:COMP, :] + force_from(product(w_ref, 0, 768, lower, PLANE), own)
        elif plane == OWN - 1:
            force = side_ref[COMP:, :] + force_from(product(w_ref, 1280, 768, upper, 0), own)
        else:
            force = force_from(after_ref[...] + product(w_ref, 640, 1408, upper, 32), own)
        for bead in range(2):
            half = momentum(plane, bead) + KICK * force[:, bead * CELLS : (bead + 1) * CELLS]
            store(plane, 1, bead, half)


def bead_kernel(map_ref, in_ref, out_ref):
    columns = []
    for r in range(9):
        columns.append(jnp.concatenate([in_ref[pl.ds(r * 4 + q, GROUP, stride=36), :] for q in range(4)], 0))
    moved = jnp.dot(
        map_ref[...],
        jnp.concatenate(columns, 1),
        precision=lax.Precision.HIGHEST,
        preferred_element_type=f32,
    )
    for r in range(9):
        line, step = r // 3, r % 3
        for q in range(4):
            row = step * 2 + q if q < 2 else 6 + (step - 1) * 2 + q - 2
            if q < 2 or step > 0:
                out_ref[pl.ds(line * 10 + row, GROUP, stride=30), :] = moved[
                    q * GROUP : (q + 1) * GROUP, r * CELLS : (r + 1) * CELLS
                ]


def last_kernel(w_ref, in_ref, pos_hbm, mom_hbm, pos_ref, mom_ref, ns, sem):
    def value(plane, kind, bead):
        half, step = place_of(plane)
        row = step * 2 + bead if kind == 0 else 6 + (step - 1) * 2 + bead
        return in_ref[pl.ds(half * 240 + row, COMP, stride=10), :]

    for plane in range(1, OWN + 1):
        for bead in range(2):
            pos_ref[pl.ds(bead * COMP * OWN + plane - 1, COMP, stride=OWN), :] = value(plane, 0, bead)
    out = pltpu.make_async_copy(pos_ref, pos_hbm, sem.at[0])
    out.start()
    clear(ns, EXT * PLANE, 32)
    for plane in range(EXT):
        for bead in range(2):
            put_neighbours(ns, plane * PLANE, bead, value(plane, 0, bead))
    for plane in range(1, OWN + 1):
        own = jnp.concatenate([value(plane, 0, bead) for bead in range(2)], 1)
        force = force_from(product(w_ref, 0, DEPTH, ns, (plane - 1) * PLANE), own)
        for bead in range(2):
            mom_ref[pl.ds(bead * COMP * OWN + plane - 1, COMP, stride=OWN), :] = (
                value(plane, 1, bead) + KICK * force[:, bead * CELLS : (bead + 1) * CELLS]
            )
    late = pltpu.make_async_copy(mom_ref, mom_hbm, sem.at[1])
    late.start()
    out.wait()
    late.wait()


def call(kernel, name, ins, outs, scratch, flops, *args, to=VMEM):
    size = sum(int(np.prod(a.shape)) * a.dtype.itemsize for a in (*args, *outs))
    return pl.pallas_call(
        kernel,
        name=name,
        in_specs=ins,
        out_specs=[to] * len(outs),
        out_shape=list(outs),
        scratch_shapes=scratch,
        compiler_params=pltpu.CompilerParams(vmem_limit_bytes=24 * 1024 * 1024),
        cost_estimate=pl.CostEstimate(flops=flops, bytes_accessed=size, transcendentals=0),
    )(*args)


def neighbours(planes, more):
    return pltpu.VMEM((planes * PLANE + more, 2 * CELLS), bf16)


def body(positions, momenta, offsets, harmonic, cubic):
    shape = jax.ShapeDtypeStruct
    per_plane = 2 * ROWS * DEPTH * 2 * CELLS
    doms = lax.axis_size("dom")
    pos = positions.reshape(2 * COMP * OWN, CELLS)
    mom = momenta.reshape(2 * COMP * OWN, CELLS)
    own = shape((2 * COMP * OWN, CELLS), f32)
    halo = shape((6 * COMP, CELLS), f32)
    (blank,) = call(tick_kernel, "blank", [], [shape((8, CELLS), f32)], [], EARLY)
    far, near, pos, mom = call(pack_kernel, "pack", [VMEM] * 3, [halo, halo, own, own], [], EARLY, blank, pos, mom)
    between = [(i, (i + 1) % doms) for i in range(1, doms, 2)]
    far = lax.ppermute(far, "dom", between + [(j, i) for i, j in between])
    near = lax.ppermute(near, "dom", [(i, i ^ 1) for i in range(doms)])
    weights, *parts = call(
        inner_kernel,
        "inner",
        [SMEM] + [VMEM] * 4,
        [shape((ROWS, DEPTH), bf16)] + [shape((n, 2 * CELLS), f32) for n in (2 * COMP, 2 * COMP, ROWS, ROWS)],
        [
            pltpu.VMEM((128, 768), f32),
            pltpu.VMEM((768, 128), f32),
            pltpu.VMEM((PLANE, 640), f32),
            pltpu.VMEM((DEPTH, 640), bf16),
            neighbours(OWN, 160),
        ],
        4 * per_plane,
        offsets,
        harmonic,
        cubic.T,
        pos,
        mom,
    )
    (send,) = call(
        outer_kernel, "outer", [VMEM] * 9, [shape((GROUP * 36, CELLS), f32)], [neighbours(2, 96)] * 2, 2 * per_plane,
        weights, pos, mom, *parts, far, near,
    )
    got = lax.all_to_all(send.reshape(GROUP, 9, 4, CELLS), "bead", 0, 0, tiled=True)
    (back,) = call(
        bead_kernel, "beads", [VMEM] * 2, [shape((GROUP * 30, CELLS), f32)], [], 2 * 64 * 64 * 9 * CELLS,
        jnp.asarray(propagator(GROUP)), got.reshape(GROUP * 36, CELLS),
    )
    got = lax.all_to_all(back.reshape(GROUP, 15, 2, CELLS), "bead", 0, 0, tiled=True)
    new_pos, new_mom = call(
        last_kernel, "last", [VMEM] * 2, [own] * 2,
        [pltpu.VMEM(own.shape, f32), pltpu.VMEM(own.shape, f32), neighbours(EXT, 32), pltpu.SemaphoreType.DMA((2,))],
        4 * per_plane, weights, got.reshape(GROUP * 30, CELLS), to=HBM,
    )
    return new_pos.reshape(positions.shape), new_mom.reshape(momenta.shape)


def solution(mesh):
    return jax.shard_map(
        body,
        mesh=mesh,
        in_specs=(P("bead", None, "dom", None), P("bead", None, "dom", None), P(), P(), P()),
        out_specs=(P("bead", None, "dom", None), P("bead", None, "dom", None)),
        check_vma=False,
    )
```

```python
import jax
import jax.numpy as jnp
import numpy as np
from jax import lax
from jax.experimental import pallas as pl
from jax.experimental.pallas import tpu as pltpu
from jax.sharding import PartitionSpec as P

BEADS = 32
COMP = 24
NOFF = 27
CZ = 16
CELLS = 128
OWN = 4
EXT = OWN + 2
NEAR = 9 * COMP
PART = 256
POINT = 2 * PART
QUAD = 4 * POINT
ROWS = 608
TIME_STEP = 0.5
CYCLE_FREQ = 1.0
KICK = 0.5 * TIME_STEP

EARLY = 10_000_000_000
GROUP = 16
HBM = pl.BlockSpec(memory_space=pltpu.HBM)
SMEM = pl.BlockSpec(memory_space=pltpu.SMEM)
VMEM = pl.BlockSpec(memory_space=pltpu.VMEM)
f32 = jnp.float32
bf16 = jnp.bfloat16


def propagator(groups):
    count = BEADS
    rows = np.arange(count)[:, None] * 1.0
    cols = np.arange(count)[None, :]
    angle = 2.0 * np.pi * rows * cols / count
    table = np.where(
        cols == 0,
        1.0 / np.sqrt(count) + 0.0 * angle,
        np.where(
            cols < count // 2,
            np.sqrt(2.0 / count) * np.cos(angle),
            np.where(
                cols == count // 2,
                np.cos(np.pi * rows) / np.sqrt(count),
                np.sqrt(2.0 / count) * np.sin(angle),
            ),
        ),
    )
    freq = 2.0 * CYCLE_FREQ * np.sin(np.pi * np.arange(count) / count)
    cosine = np.cos(freq * TIME_STEP)
    sine_over = np.where(
        freq > 0, np.sin(freq * TIME_STEP) / np.where(freq > 0, freq, 1.0), TIME_STEP
    )
    spring = freq * np.sin(freq * TIME_STEP)
    turn = (table * cosine) @ table.T
    drift = (table * sine_over) @ table.T
    pull = (table * spring) @ table.T
    whole = np.block([[turn, drift], [-pull, turn]])
    per = count // groups
    order = np.arange(2 * count).reshape(2, groups, per).transpose(0, 2, 1).reshape(-1)
    return whole[np.ix_(order, order)].astype(np.float32)


def put_neighbours(ns_ref, row, bead, field):
    z = lax.broadcasted_iota(jnp.int32, field.shape, 1) % CZ
    up = jnp.where(z == CZ - 1, pltpu.roll(field, CZ - 1, 1), pltpu.roll(field, CELLS - 1, 1))
    down = jnp.where(z == 0, pltpu.roll(field, CELLS - CZ + 1, 1), pltpu.roll(field, 1, 1))
    along_z = [down, field, up]
    parts = [pltpu.roll(v, CZ, 1) for v in along_z]
    parts += along_z
    parts += [pltpu.roll(v, CELLS - CZ, 1) for v in along_z]
    parts.append(jnp.zeros((PART - NEAR, CELLS), f32))
    stack = jnp.concatenate(parts, 0)
    high = stack.astype(bf16)
    low = (stack - high.astype(f32)).astype(bf16)
    lanes = pl.ds(bead * CELLS, CELLS)
    ns_ref[pl.ds(row, PART), lanes] = low
    ns_ref[pl.ds(row + PART, PART), lanes] = high


def put_quad(ns_ref, row, fields):
    for bead in range(2):
        d0, d1, d2, d3 = (plane[bead] for plane in fields)
        for q, field in enumerate((d0 - d2, d1 + d2, d2 - d1, d1 - d3)):
            put_neighbours(ns_ref, row + q * POINT, bead, field)


def two_rows(w_ref, ns_ref, row):
    m = []
    for q in range(4):
        high = jnp.dot(
            w_ref[:, q * POINT : q * POINT + PART],
            ns_ref[pl.ds(row + q * POINT + PART, PART), :],
            preferred_element_type=f32,
        )
        rest = jnp.dot(
            w_ref[:, q * POINT : (q + 1) * POINT],
            ns_ref[pl.ds(row + q * POINT, POINT), :],
            preferred_element_type=f32,
        )
        m.append(high + rest)
    return m[0] + (m[1] + m[2]), (m[1] - m[2]) - m[3]


def force_from(rows, own):
    higher = rows[: COMP * COMP].reshape(COMP, COMP, 2 * CELLS)
    anharm = jnp.sum(higher * own[None, :, :], axis=1)
    return -(rows[COMP * COMP : COMP * COMP + COMP] + anharm)


def halves(core, here, there):
    return jnp.where(core == 0, here, there)


def own_plane(ref, bead, plane):
    return ref[pl.ds(bead * COMP * OWN + plane, COMP, stride=OWN), :]


def block(ref, place, bead):
    return ref[(place * 2 + bead) * COMP : (place * 2 + bead + 1) * COMP, :]


def pair(ref, place):
    return jnp.concatenate([block(ref, place, bead) for bead in range(2)], 1)


def clear(ref, row, count):
    ref[row : row + count, :] = jnp.zeros((count, ref.shape[1]), ref.dtype)


def tick_kernel(out_ref):
    clear(out_ref, 0, 8)


def planes_kernel(ref, planes_ref):
    for plane in range(OWN):
        for bead in range(2):
            planes_ref[pl.ds((plane * 2 + bead) * COMP, COMP), :] = own_plane(ref, bead, plane)


def pack_kernel(blank_ref, raw_pos_ref, raw_mom_ref, far_ref, near_ref, pos_ref, mom_ref):
    core = lax.axis_index("dom") % 2
    planes_kernel(raw_pos_ref, pos_ref)
    planes_kernel(raw_mom_ref, mom_ref)
    for bead in range(2):
        pos = [own_plane(raw_pos_ref, bead, plane) for plane in range(OWN)]
        first, last = (own_plane(raw_mom_ref, bead, plane) for plane in (0, OWN - 1))
        for place, left, right in ((0, pos[0], pos[2]), (1, pos[1], pos[3]), (2, first, last)):
            rows = pl.ds((place * 2 + bead) * COMP, COMP)
            far_ref[rows, :] = halves(core, left, right)
            near_ref[rows, :] = halves(core, right, left)


def inner_kernel(off_ref, harm_ref, cub_ref, pos_ref, mom_ref, w_ref, half_ref, hpad, hturn, wt, cat, ns):
    put_quad(ns, 0, [[block(pos_ref, plane, bead) for bead in range(2)] for plane in range(OWN)])
    hpad[...] = jnp.zeros_like(hpad)
    hpad[64 : 64 + COMP, 0 : NOFF * COMP] = harm_ref[...]
    for tile in range(6):
        hturn[tile * 128 : (tile + 1) * 128, :] = hpad[:, tile * 128 : (tile + 1) * 128].T
    for o in range(NOFF):
        rows = pl.ds(pl.multiple_of(off_ref[o] * COMP, 8), COMP)
        wt[rows, 512:640] = hturn[o * COMP : (o + 1) * COMP, :]
        wt[rows, 0 : COMP * COMP] = cub_ref[o * COMP : (o + 1) * COMP, :]
    before, here, after = (wt[dx * NEAR : (dx + 1) * NEAR, :] for dx in range(3))
    outer = before + after
    for q, weight in enumerate((before, 0.5 * (outer + here), 0.5 * (outer - here), after)):
        weight = jnp.concatenate([weight, jnp.zeros((PART - NEAR, 640), f32)], 0)
        high = weight.astype(bf16)
        cat[q * POINT : q * POINT + PART, :] = high
        cat[q * POINT + PART : (q + 1) * POINT, :] = (weight - high.astype(f32)).astype(bf16)
    for m in range(5):
        size = min(128, ROWS - m * 128)
        for k in range(QUAD // 128):
            turned = cat[k * 128 : (k + 1) * 128, m * 128 : (m + 1) * 128].T
            w_ref[m * 128 : m * 128 + size, k * 128 : (k + 1) * 128] = turned[:size]
    for plane, rows in zip((1, 2), two_rows(w_ref, ns, 0)):
        force = force_from(rows, pair(pos_ref, plane))
        half_ref[(plane - 1) * COMP : plane * COMP, :] = pair(mom_ref, plane) + KICK * force


def place_of(plane):
    return (0, plane) if plane < 3 else (1, EXT - 1 - plane)


def outer_kernel(w_ref, pos_ref, mom_ref, half_ref, far_ref, near_ref, send_ref, ns):
    core = lax.axis_index("dom") % 2
    left = [[halves(core, block(far_ref, i, bead), block(near_ref, i, bead)) for bead in range(2)] for i in range(3)]
    right = [[halves(core, block(near_ref, i, bead), block(far_ref, i, bead)) for bead in range(2)] for i in range(3)]

    def position(plane, bead):
        if plane < 0:
            return left[plane + 2][bead]
        if plane >= OWN:
            return right[plane - OWN][bead]
        return block(pos_ref, plane, bead)

    def momentum(plane, bead):
        if plane < 0:
            return left[2][bead]
        if plane >= OWN:
            return right[2][bead]
        return block(mom_ref, plane, bead)

    def store(plane, kind, bead, value):
        half, step = place_of(plane + 1)
        send_ref[pl.ds(half * 288 + step * 4 + kind * 2 + bead, COMP, stride=12), :] = value

    for i, first in enumerate((-1, OWN - 1)):
        put_quad(ns, i * QUAD, [[position(first + n, bead) for bead in range(2)] for n in range(-1, 3)])
    for plane in range(-1, OWN + 1):
        for bead in range(2):
            store(plane, 0, bead, position(plane, bead))
    for plane in (1, 2):
        for bead in range(2):
            store(plane, 1, bead, half_ref[(plane - 1) * COMP : plane * COMP, bead * CELLS : (bead + 1) * CELLS])
    for i, first in enumerate((-1, OWN - 1)):
        for plane, rows in zip((first, first + 1), two_rows(w_ref, ns, i * QUAD)):
            force = force_from(rows, jnp.concatenate([position(plane, bead) for bead in range(2)], 1))
            for bead in range(2):
                half = momentum(plane, bead) + KICK * force[:, bead * CELLS : (bead + 1) * CELLS]
                store(plane, 1, bead, half)


def bead_kernel(map_ref, in_ref, out_ref):
    columns = []
    for r in range(9):
        columns.append(jnp.concatenate([in_ref[pl.ds(r * 4 + q, GROUP, stride=36), :] for q in range(4)], 0))
    moved = jnp.dot(
        map_ref[...],
        jnp.concatenate(columns, 1),
        precision=lax.Precision.HIGHEST,
        preferred_element_type=f32,
    )
    for r in range(9):
        line, step = r // 3, r % 3
        for q in range(4):
            row = step * 2 + q if q < 2 else 6 + (step - 1) * 2 + q - 2
            if q < 2 or step > 0:
                out_ref[pl.ds(line * 10 + row, GROUP, stride=30), :] = moved[
                    q * GROUP : (q + 1) * GROUP, r * CELLS : (r + 1) * CELLS
                ]


def last_kernel(w_ref, in_ref, pos_hbm, mom_hbm, pos_ref, mom_ref, ns, sem):
    def value(plane, kind, bead):
        half, step = place_of(plane)
        row = step * 2 + bead if kind == 0 else 6 + (step - 1) * 2 + bead
        return in_ref[pl.ds(half * 240 + row, COMP, stride=10), :]

    for plane in range(1, OWN + 1):
        for bead in range(2):
            pos_ref[pl.ds(bead * COMP * OWN + plane - 1, COMP, stride=OWN), :] = value(plane, 0, bead)
    out = pltpu.make_async_copy(pos_ref, pos_hbm, sem.at[0])
    out.start()
    for i, first in enumerate((1, 3)):
        put_quad(ns, i * QUAD, [[value(first + n, 0, bead) for bead in range(2)] for n in range(-1, 3)])
    for i, first in enumerate((1, 3)):
        for plane, rows in zip((first, first + 1), two_rows(w_ref, ns, i * QUAD)):
            force = force_from(rows, jnp.concatenate([value(plane, 0, bead) for bead in range(2)], 1))
            for bead in range(2):
                mom_ref[pl.ds(bead * COMP * OWN + plane - 1, COMP, stride=OWN), :] = (
                    value(plane, 1, bead) + KICK * force[:, bead * CELLS : (bead + 1) * CELLS]
                )
    late = pltpu.make_async_copy(mom_ref, mom_hbm, sem.at[1])
    late.start()
    out.wait()
    late.wait()


def call(kernel, name, ins, outs, scratch, flops, *args, to=VMEM):
    size = sum(int(np.prod(a.shape)) * a.dtype.itemsize for a in (*args, *outs))
    return pl.pallas_call(
        kernel,
        name=name,
        in_specs=ins,
        out_specs=[to] * len(outs),
        out_shape=list(outs),
        scratch_shapes=scratch,
        compiler_params=pltpu.CompilerParams(vmem_limit_bytes=24 * 1024 * 1024),
        cost_estimate=pl.CostEstimate(flops=flops, bytes_accessed=size, transcendentals=0),
    )(*args)


def neighbours(quads):
    return pltpu.VMEM((quads * QUAD, 2 * CELLS), bf16)


def body(positions, momenta, offsets, harmonic, cubic):
    shape = jax.ShapeDtypeStruct
    per_plane = 2 * ROWS * (QUAD * 3 // 4) * 2 * CELLS
    doms = lax.axis_size("dom")
    pos = positions.reshape(2 * COMP * OWN, CELLS)
    mom = momenta.reshape(2 * COMP * OWN, CELLS)
    own = shape((2 * COMP * OWN, CELLS), f32)
    halo = shape((6 * COMP, CELLS), f32)
    (blank,) = call(tick_kernel, "blank", [], [shape((8, CELLS), f32)], [], EARLY)
    far, near, pos, mom = call(pack_kernel, "pack", [VMEM] * 3, [halo, halo, own, own], [], EARLY, blank, pos, mom)
    between = [(i, (i + 1) % doms) for i in range(1, doms, 2)]
    far = lax.ppermute(far, "dom", between + [(j, i) for i, j in between])
    near = lax.ppermute(near, "dom", [(i, i ^ 1) for i in range(doms)])
    weights, half = call(
        inner_kernel,
        "inner",
        [SMEM] + [VMEM] * 4,
        [shape((ROWS, QUAD), bf16), shape((2 * COMP, 2 * CELLS), f32)],
        [
            pltpu.VMEM((128, 768), f32),
            pltpu.VMEM((768, 128), f32),
            pltpu.VMEM((3 * NEAR, 640), f32),
            pltpu.VMEM((QUAD, 640), bf16),
            neighbours(1),
        ],
        2 * per_plane,
        offsets,
        harmonic,
        cubic.T,
        pos,
        mom,
    )
    (send,) = call(
        outer_kernel, "outer", [VMEM] * 6, [shape((GROUP * 36, CELLS), f32)], [neighbours(2)], 4 * per_plane,
        weights, pos, mom, half, far, near,
    )
    got = lax.all_to_all(send.reshape(GROUP, 9, 4, CELLS), "bead", 0, 0, tiled=True)
    (back,) = call(
        bead_kernel, "beads", [VMEM] * 2, [shape((GROUP * 30, CELLS), f32)], [], 2 * 64 * 64 * 9 * CELLS,
        jnp.asarray(propagator(GROUP)), got.reshape(GROUP * 36, CELLS),
    )
    got = lax.all_to_all(back.reshape(GROUP, 15, 2, CELLS), "bead", 0, 0, tiled=True)
    new_pos, new_mom = call(
        last_kernel, "last", [VMEM] * 2, [own] * 2,
        [pltpu.VMEM(own.shape, f32), pltpu.VMEM(own.shape, f32), neighbours(2), pltpu.SemaphoreType.DMA((2,))],
        4 * per_plane, weights, got.reshape(GROUP * 30, CELLS), to=HBM,
    )
    return new_pos.reshape(positions.shape), new_mom.reshape(momenta.shape)


def solution(mesh):
    return jax.shard_map(
        body,
        mesh=mesh,
        in_specs=(P("bead", None, "dom", None), P("bead", None, "dom", None), P(), P(), P()),
        out_specs=(P("bead", None, "dom", None), P("bead", None, "dom", None)),
        check_vma=False,
    )
```

```python
import jax
import jax.numpy as jnp
import numpy as np
from jax import lax
from jax.experimental import pallas as pl
from jax.experimental.pallas import tpu as pltpu
from jax.sharding import PartitionSpec as P

BEADS = 32
COMP = 24
NOFF = 27
CZ = 16
CELLS = 128
OWN = 4
EXT = OWN + 2
NEAR = 9 * COMP
PART = 256
POINT = 2 * PART
QUAD = 4 * POINT
ROWS = 608
TIME_STEP = 0.5
CYCLE_FREQ = 1.0
KICK = 0.5 * TIME_STEP

EARLY = 10_000_000_000
GROUP = 16
HBM = pl.BlockSpec(memory_space=pltpu.HBM)
SMEM = pl.BlockSpec(memory_space=pltpu.SMEM)
VMEM = pl.BlockSpec(memory_space=pltpu.VMEM)
f32 = jnp.float32
bf16 = jnp.bfloat16


def propagator(groups):
    count = BEADS
    rows = np.arange(count)[:, None] * 1.0
    cols = np.arange(count)[None, :]
    angle = 2.0 * np.pi * rows * cols / count
    table = np.where(
        cols == 0,
        1.0 / np.sqrt(count) + 0.0 * angle,
        np.where(
            cols < count // 2,
            np.sqrt(2.0 / count) * np.cos(angle),
            np.where(
                cols == count // 2,
                np.cos(np.pi * rows) / np.sqrt(count),
                np.sqrt(2.0 / count) * np.sin(angle),
            ),
        ),
    )
    freq = 2.0 * CYCLE_FREQ * np.sin(np.pi * np.arange(count) / count)
    cosine = np.cos(freq * TIME_STEP)
    sine_over = np.where(
        freq > 0, np.sin(freq * TIME_STEP) / np.where(freq > 0, freq, 1.0), TIME_STEP
    )
    spring = freq * np.sin(freq * TIME_STEP)
    turn = (table * cosine) @ table.T
    drift = (table * sine_over) @ table.T
    pull = (table * spring) @ table.T
    whole = np.block([[turn, drift], [-pull, turn]])
    per = count // groups
    order = np.arange(2 * count).reshape(2, groups, per).transpose(0, 2, 1).reshape(-1)
    return whole[np.ix_(order, order)].astype(np.float32)


def put_neighbours(ns_ref, row, bead, field):
    z = lax.broadcasted_iota(jnp.int32, field.shape, 1) % CZ
    up = jnp.where(z == CZ - 1, pltpu.roll(field, CZ - 1, 1), pltpu.roll(field, CELLS - 1, 1))
    down = jnp.where(z == 0, pltpu.roll(field, CELLS - CZ + 1, 1), pltpu.roll(field, 1, 1))
    along_z = [down, field, up]
    parts = [pltpu.roll(v, CZ, 1) for v in along_z]
    parts += along_z
    parts += [pltpu.roll(v, CELLS - CZ, 1) for v in along_z]
    parts.append(jnp.zeros((PART - NEAR, CELLS), f32))
    stack = jnp.concatenate(parts, 0)
    high = stack.astype(bf16)
    low = (stack - high.astype(f32)).astype(bf16)
    lanes = pl.ds(bead * CELLS, CELLS)
    ns_ref[pl.ds(row, PART), lanes] = low
    ns_ref[pl.ds(row + PART, PART), lanes] = high


def put_quad(ns_ref, row, fields):
    for bead in range(2):
        d0, d1, d2, d3 = (plane[bead] for plane in fields)
        for q, field in enumerate((d0 - d2, d1 + d2, d2 - d1, d1 - d3)):
            put_neighbours(ns_ref, row + q * POINT, bead, field)


def two_rows(w_ref, ns_ref, row):
    m = []
    for q in range(4):
        high = jnp.dot(
            w_ref[:, q * POINT : q * POINT + PART],
            ns_ref[pl.ds(row + q * POINT + PART, PART), :],
            preferred_element_type=f32,
        )
        rest = jnp.dot(
            w_ref[:, q * POINT : (q + 1) * POINT],
            ns_ref[pl.ds(row + q * POINT, POINT), :],
            preferred_element_type=f32,
        )
        m.append(high + rest)
    return m[0] + (m[1] + m[2]), (m[1] - m[2]) - m[3]


def force_from(rows, own):
    higher = rows[: COMP * COMP].reshape(COMP, COMP, 2 * CELLS)
    anharm = jnp.sum(higher * own[None, :, :], axis=1)
    return -(rows[COMP * COMP : COMP * COMP + COMP] + anharm)


def halves(core, here, there):
    return jnp.where(core == 0, here, there)


def own_plane(ref, bead, plane):
    return ref[pl.ds(bead * COMP * OWN + plane, COMP, stride=OWN), :]


def block(ref, place, bead):
    return ref[(place * 2 + bead) * COMP : (place * 2 + bead + 1) * COMP, :]


def pair(ref, place):
    return jnp.concatenate([block(ref, place, bead) for bead in range(2)], 1)


def clear(ref, row, count):
    ref[row : row + count, :] = jnp.zeros((count, ref.shape[1]), ref.dtype)


def tick_kernel(out_ref):
    clear(out_ref, 0, 8)


def planes_kernel(ref, planes_ref):
    for plane in range(OWN):
        for bead in range(2):
            planes_ref[pl.ds((plane * 2 + bead) * COMP, COMP), :] = own_plane(ref, bead, plane)


def pack_kernel(blank_ref, raw_pos_ref, raw_mom_ref, far_ref, near_ref, pos_ref, mom_ref):
    core = lax.axis_index("dom") % 2
    planes_kernel(raw_pos_ref, pos_ref)
    planes_kernel(raw_mom_ref, mom_ref)
    for bead in range(2):
        pos = [own_plane(raw_pos_ref, bead, plane) for plane in range(OWN)]
        first, last = (own_plane(raw_mom_ref, bead, plane) for plane in (0, OWN - 1))
        for place, left, right in ((0, pos[0], pos[2]), (1, pos[1], pos[3]), (2, first, last)):
            rows = pl.ds((place * 2 + bead) * COMP, COMP)
            far_ref[rows, :] = halves(core, left, right)
            near_ref[rows, :] = halves(core, right, left)


def inner_kernel(off_ref, harm_ref, cub_ref, pos_ref, mom_ref, w_ref, half_ref, order, hpad, tail, cat, ns):
    put_quad(ns, 0, [[block(pos_ref, plane, bead) for bead in range(2)] for plane in range(OWN)])
    for o in range(NOFF):
        order[o] = 0
    for o in range(NOFF):
        order[off_ref[o]] = o
    clear(hpad, 0, 128)
    hpad[64 : 64 + COMP, 0 : NOFF * COMP] = harm_ref[...]
    for tile in range(6):
        tail[tile * 128 : (tile + 1) * 128, :] = hpad[:, tile * 128 : (tile + 1) * 128].T
    tail[0 : NOFF * COMP, 0:64] = cub_ref[:, 512 : COMP * COMP]

    def weights_of(code):
        rows = pl.ds(pl.multiple_of(order[code] * COMP, 8), COMP)
        return jnp.concatenate([cub_ref[rows, 0:512], tail[rows, :]], 1)

    for s in range(0, 9, 2):
        shifts = range(s, min(s + 2, 9))
        before, here, after = (
            jnp.concatenate([weights_of(dx * 9 + shift) for shift in shifts], 0) for dx in range(3)
        )
        outer = before + after
        for q, weight in enumerate((before, 0.5 * (outer + here), 0.5 * (outer - here), after)):
            if len(shifts) == 1:
                weight = jnp.concatenate([weight, jnp.zeros((PART - NEAR, 640), f32)], 0)
            high = weight.astype(bf16)
            rows = pl.ds(q * POINT + s * COMP, weight.shape[0])
            cat[rows, :] = high
            rows = pl.ds(q * POINT + PART + s * COMP, weight.shape[0])
            cat[rows, :] = (weight - high.astype(f32)).astype(bf16)
    for m in range(0, ROWS, 128):
        size = min(128, ROWS - m)
        for k in range(0, QUAD, 128):
            w_ref[m : m + size, k : k + 128] = cat[k : k + 128, m : m + 128].T[:size]
    for plane, rows in zip((1, 2), two_rows(w_ref, ns, 0)):
        force = force_from(rows, pair(pos_ref, plane))
        half_ref[(plane - 1) * COMP : plane * COMP, :] = pair(mom_ref, plane) + KICK * force


def place_of(plane):
    return (0, plane) if plane < 3 else (1, EXT - 1 - plane)


def outer_kernel(w_ref, pos_ref, mom_ref, half_ref, far_ref, near_ref, send_ref, ns):
    core = lax.axis_index("dom") % 2
    left = [[halves(core, block(far_ref, i, bead), block(near_ref, i, bead)) for bead in range(2)] for i in range(3)]
    right = [[halves(core, block(near_ref, i, bead), block(far_ref, i, bead)) for bead in range(2)] for i in range(3)]

    def position(plane, bead):
        if plane < 0:
            return left[plane + 2][bead]
        if plane >= OWN:
            return right[plane - OWN][bead]
        return block(pos_ref, plane, bead)

    def momentum(plane, bead):
        if plane < 0:
            return left[2][bead]
        if plane >= OWN:
            return right[2][bead]
        return block(mom_ref, plane, bead)

    def store(plane, kind, bead, value):
        half, step = place_of(plane + 1)
        send_ref[pl.ds(half * 288 + step * 4 + kind * 2 + bead, COMP, stride=12), :] = value

    for i, first in enumerate((-1, OWN - 1)):
        put_quad(ns, i * QUAD, [[position(first + n, bead) for bead in range(2)] for n in range(-1, 3)])
    for plane in range(-1, OWN + 1):
        for bead in range(2):
            store(plane, 0, bead, position(plane, bead))
    for plane in (1, 2):
        for bead in range(2):
            store(plane, 1, bead, half_ref[(plane - 1) * COMP : plane * COMP, bead * CELLS : (bead + 1) * CELLS])
    for i, first in enumerate((-1, OWN - 1)):
        for plane, rows in zip((first, first + 1), two_rows(w_ref, ns, i * QUAD)):
            force = force_from(rows, jnp.concatenate([position(plane, bead) for bead in range(2)], 1))
            for bead in range(2):
                half = momentum(plane, bead) + KICK * force[:, bead * CELLS : (bead + 1) * CELLS]
                store(plane, 1, bead, half)


def bead_kernel(map_ref, in_ref, out_ref):
    columns = []
    for r in range(9):
        columns.append(jnp.concatenate([in_ref[pl.ds(r * 4 + q, GROUP, stride=36), :] for q in range(4)], 0))
    moved = jnp.dot(
        map_ref[...],
        jnp.concatenate(columns, 1),
        precision=lax.Precision.HIGHEST,
        preferred_element_type=f32,
    )
    for r in range(9):
        line, step = r // 3, r % 3
        for q in range(4):
            row = step * 2 + q if q < 2 else 6 + (step - 1) * 2 + q - 2
            if q < 2 or step > 0:
                out_ref[pl.ds(line * 10 + row, GROUP, stride=30), :] = moved[
                    q * GROUP : (q + 1) * GROUP, r * CELLS : (r + 1) * CELLS
                ]


def last_kernel(w_ref, in_ref, pos_hbm, mom_hbm, pos_ref, mom_ref, ns, sem):
    def value(plane, kind, bead):
        half, step = place_of(plane)
        row = step * 2 + bead if kind == 0 else 6 + (step - 1) * 2 + bead
        return in_ref[pl.ds(half * 240 + row, COMP, stride=10), :]

    for plane in range(1, OWN + 1):
        for bead in range(2):
            pos_ref[pl.ds(bead * COMP * OWN + plane - 1, COMP, stride=OWN), :] = value(plane, 0, bead)
    out = pltpu.make_async_copy(pos_ref, pos_hbm, sem.at[0])
    out.start()
    for i, first in enumerate((1, 3)):
        put_quad(ns, i * QUAD, [[value(first + n, 0, bead) for bead in range(2)] for n in range(-1, 3)])
    for i, first in enumerate((1, 3)):
        for plane, rows in zip((first, first + 1), two_rows(w_ref, ns, i * QUAD)):
            force = force_from(rows, jnp.concatenate([value(plane, 0, bead) for bead in range(2)], 1))
            for bead in range(2):
                mom_ref[pl.ds(bead * COMP * OWN + plane - 1, COMP, stride=OWN), :] = (
                    value(plane, 1, bead) + KICK * force[:, bead * CELLS : (bead + 1) * CELLS]
                )
    late = pltpu.make_async_copy(mom_ref, mom_hbm, sem.at[1])
    late.start()
    out.wait()
    late.wait()


def call(kernel, name, ins, outs, scratch, flops, *args, to=VMEM):
    size = sum(int(np.prod(a.shape)) * a.dtype.itemsize for a in (*args, *outs))
    return pl.pallas_call(
        kernel,
        name=name,
        in_specs=ins,
        out_specs=[to] * len(outs),
        out_shape=list(outs),
        scratch_shapes=scratch,
        compiler_params=pltpu.CompilerParams(vmem_limit_bytes=24 * 1024 * 1024),
        cost_estimate=pl.CostEstimate(flops=flops, bytes_accessed=size, transcendentals=0),
    )(*args)


def neighbours(quads):
    return pltpu.VMEM((quads * QUAD, 2 * CELLS), bf16)


def body(positions, momenta, offsets, harmonic, cubic):
    shape = jax.ShapeDtypeStruct
    per_plane = 2 * ROWS * (QUAD * 3 // 4) * 2 * CELLS
    doms = lax.axis_size("dom")
    pos = positions.reshape(2 * COMP * OWN, CELLS)
    mom = momenta.reshape(2 * COMP * OWN, CELLS)
    own = shape((2 * COMP * OWN, CELLS), f32)
    halo = shape((6 * COMP, CELLS), f32)
    (blank,) = call(tick_kernel, "blank", [], [shape((8, CELLS), f32)], [], EARLY)
    far, near, pos, mom = call(pack_kernel, "pack", [VMEM] * 3, [halo, halo, own, own], [], EARLY, blank, pos, mom)
    between = [(i, (i + 1) % doms) for i in range(1, doms, 2)]
    far = lax.ppermute(far, "dom", between + [(j, i) for i, j in between])
    near = lax.ppermute(near, "dom", [(i, i ^ 1) for i in range(doms)])
    weights, half = call(
        inner_kernel,
        "inner",
        [SMEM] + [VMEM] * 4,
        [shape((ROWS, QUAD), bf16), shape((2 * COMP, 2 * CELLS), f32)],
        [
            pltpu.SMEM((NOFF,), jnp.int32),
            pltpu.VMEM((128, 768), f32),
            pltpu.VMEM((768, 128), f32),
            pltpu.VMEM((QUAD, 640), bf16),
            neighbours(1),
        ],
        2 * per_plane,
        offsets,
        harmonic,
        cubic.T,
        pos,
        mom,
    )
    (send,) = call(
        outer_kernel, "outer", [VMEM] * 6, [shape((GROUP * 36, CELLS), f32)], [neighbours(2)], 4 * per_plane,
        weights, pos, mom, half, far, near,
    )
    got = lax.all_to_all(send.reshape(GROUP, 9, 4, CELLS), "bead", 0, 0, tiled=True)
    (back,) = call(
        bead_kernel, "beads", [VMEM] * 2, [shape((GROUP * 30, CELLS), f32)], [], 2 * 64 * 64 * 9 * CELLS,
        jnp.asarray(propagator(GROUP)), got.reshape(GROUP * 36, CELLS),
    )
    got = lax.all_to_all(back.reshape(GROUP, 15, 2, CELLS), "bead", 0, 0, tiled=True)
    new_pos, new_mom = call(
        last_kernel, "last", [VMEM] * 2, [own] * 2,
        [pltpu.VMEM(own.shape, f32), pltpu.VMEM(own.shape, f32), neighbours(2), pltpu.SemaphoreType.DMA((2,))],
        4 * per_plane, weights, got.reshape(GROUP * 30, CELLS), to=HBM,
    )
    return new_pos.reshape(positions.shape), new_mom.reshape(momenta.shape)


def solution(mesh):
    return jax.shard_map(
        body,
        mesh=mesh,
        in_specs=(P("bead", None, "dom", None), P("bead", None, "dom", None), P(), P(), P()),
        out_specs=(P("bead", None, "dom", None), P("bead", None, "dom", None)),
        check_vma=False,
    )
```

```python
import jax
import jax.numpy as jnp
import numpy as np
from jax import lax
from jax.experimental import pallas as pl
from jax.experimental.pallas import tpu as pltpu
from jax.sharding import PartitionSpec as P

BEADS = 32
COMP = 24
NOFF = 27
CZ = 16
CELLS = 128
OWN = 4
EXT = OWN + 2
NEAR = 9 * COMP
PART = 256
POINT = 2 * PART
QUAD = 4 * POINT
ROWS = 608
TIME_STEP = 0.5
CYCLE_FREQ = 1.0
KICK = 0.5 * TIME_STEP

EARLY = 10_000_000_000
GROUP = 16
HBM = pl.BlockSpec(memory_space=pltpu.HBM)
SMEM = pl.BlockSpec(memory_space=pltpu.SMEM)
VMEM = pl.BlockSpec(memory_space=pltpu.VMEM)
f32 = jnp.float32
bf16 = jnp.bfloat16


def propagator(groups):
    count = BEADS
    rows = np.arange(count)[:, None] * 1.0
    cols = np.arange(count)[None, :]
    angle = 2.0 * np.pi * rows * cols / count
    table = np.where(
        cols == 0,
        1.0 / np.sqrt(count) + 0.0 * angle,
        np.where(
            cols < count // 2,
            np.sqrt(2.0 / count) * np.cos(angle),
            np.where(
                cols == count // 2,
                np.cos(np.pi * rows) / np.sqrt(count),
                np.sqrt(2.0 / count) * np.sin(angle),
            ),
        ),
    )
    freq = 2.0 * CYCLE_FREQ * np.sin(np.pi * np.arange(count) / count)
    cosine = np.cos(freq * TIME_STEP)
    sine_over = np.where(
        freq > 0, np.sin(freq * TIME_STEP) / np.where(freq > 0, freq, 1.0), TIME_STEP
    )
    spring = freq * np.sin(freq * TIME_STEP)
    turn = (table * cosine) @ table.T
    drift = (table * sine_over) @ table.T
    pull = (table * spring) @ table.T
    whole = np.block([[turn, drift], [-pull, turn]])
    per = count // groups
    order = np.arange(2 * count).reshape(2, groups, per).transpose(0, 2, 1).reshape(-1)
    return whole[np.ix_(order, order)].astype(np.float32)


def neighbours(field):
    z = lax.broadcasted_iota(jnp.int32, field.shape, 1) % CZ
    up = jnp.where(z == CZ - 1, pltpu.roll(field, CZ - 1, 1), pltpu.roll(field, CELLS - 1, 1))
    down = jnp.where(z == 0, pltpu.roll(field, CELLS - CZ + 1, 1), pltpu.roll(field, 1, 1))
    along_z = [down, field, up]
    parts = [pltpu.roll(v, CZ, 1) for v in along_z]
    parts += along_z
    parts += [pltpu.roll(v, CELLS - CZ, 1) for v in along_z]
    parts.append(jnp.zeros((PART - NEAR, CELLS), f32))
    stack = jnp.concatenate(parts, 0)
    high = stack.astype(bf16)
    return (stack - high.astype(f32)).astype(bf16), high


def two_rows(w_ref, fields):
    sums = []
    for bead in range(2):
        d0, d1, d2, d3 = (plane[bead] for plane in fields)
        sums.append((d0 - d2, d1 + d2, d2 - d1, d1 - d3))
    m = []
    for q in range(4):
        low, high = (jnp.concatenate(parts, 1) for parts in zip(*(neighbours(sums[bead][q]) for bead in range(2))))
        whole = jnp.dot(w_ref[:, q * POINT : q * POINT + PART], high, preferred_element_type=f32)
        rest = jnp.dot(
            w_ref[:, q * POINT : (q + 1) * POINT], jnp.concatenate([low, high], 0), preferred_element_type=f32
        )
        m.append(whole + rest)
    return m[0] + (m[1] + m[2]), (m[1] - m[2]) - m[3]


def force_from(rows, own):
    higher = rows[: COMP * COMP].reshape(COMP, COMP, 2 * CELLS)
    anharm = jnp.sum(higher * own[None, :, :], axis=1)
    return -(rows[COMP * COMP : COMP * COMP + COMP] + anharm)


def halves(core, here, there):
    return jnp.where(core == 0, here, there)


def own_plane(ref, bead, plane):
    return ref[pl.ds(bead * COMP * OWN + plane, COMP, stride=OWN), :]


def block(ref, place, bead):
    return ref[(place * 2 + bead) * COMP : (place * 2 + bead + 1) * COMP, :]


def pair(ref, place):
    return jnp.concatenate([block(ref, place, bead) for bead in range(2)], 1)


def clear(ref, row, count):
    ref[row : row + count, :] = jnp.zeros((count, ref.shape[1]), ref.dtype)


def tick_kernel(out_ref):
    clear(out_ref, 0, 8)


def planes_kernel(ref, planes_ref):
    for plane in range(OWN):
        for bead in range(2):
            planes_ref[pl.ds((plane * 2 + bead) * COMP, COMP), :] = own_plane(ref, bead, plane)


def pack_kernel(blank_ref, raw_pos_ref, raw_mom_ref, far_ref, near_ref, pos_ref, mom_ref):
    core = lax.axis_index("dom") % 2
    planes_kernel(raw_pos_ref, pos_ref)
    planes_kernel(raw_mom_ref, mom_ref)
    for bead in range(2):
        pos = [own_plane(raw_pos_ref, bead, plane) for plane in range(OWN)]
        first, last = (own_plane(raw_mom_ref, bead, plane) for plane in (0, OWN - 1))
        for place, left, right in ((0, pos[0], pos[2]), (1, pos[1], pos[3]), (2, first, last)):
            rows = pl.ds((place * 2 + bead) * COMP, COMP)
            far_ref[rows, :] = halves(core, left, right)
            near_ref[rows, :] = halves(core, right, left)


def inner_kernel(off_ref, harm_ref, cub_ref, pos_ref, mom_ref, w_ref, half_ref, order, hpad, tail):
    fields = [[block(pos_ref, plane, bead) for bead in range(2)] for plane in range(OWN)]
    for o in range(NOFF):
        order[o] = 0
    for o in range(NOFF):
        order[off_ref[o]] = o
    clear(hpad, 0, 128)
    hpad[64 : 64 + COMP, 0 : NOFF * COMP] = harm_ref[...]
    for tile in range(6):
        tail[tile * 128 : (tile + 1) * 128, :] = hpad[:, tile * 128 : (tile + 1) * 128].T
    tail[0 : NOFF * COMP, 0:64] = cub_ref[:, 512 : COMP * COMP]

    def weights_of(code):
        rows = pl.ds(pl.multiple_of(order[code] * COMP, 8), COMP)
        return jnp.concatenate([cub_ref[rows, 0:512], tail[rows, :]], 1)

    points = [[] for _ in range(8)]
    for s in range(0, 9, 2):
        shifts = range(s, min(s + 2, 9))
        before, here, after = (
            jnp.concatenate([weights_of(dx * 9 + shift) for shift in shifts], 0) for dx in range(3)
        )
        outer = before + after
        for q, weight in enumerate((before, 0.5 * (outer + here), 0.5 * (outer - here), after)):
            if len(shifts) == 1:
                weight = jnp.concatenate([weight, jnp.zeros((PART - NEAR, 640), f32)], 0)
            high = weight.astype(bf16)
            points[2 * q].append(high)
            points[2 * q + 1].append((weight - high.astype(f32)).astype(bf16))
    for i, parts in enumerate(points):
        w_ref[:, i * PART : (i + 1) * PART] = jnp.concatenate(parts, 0).T[:ROWS]
    for plane, rows in zip((1, 2), two_rows(w_ref, fields)):
        force = force_from(rows, pair(pos_ref, plane))
        half_ref[(plane - 1) * COMP : plane * COMP, :] = pair(mom_ref, plane) + KICK * force


def place_of(plane):
    return (0, plane) if plane < 3 else (1, EXT - 1 - plane)


def outer_kernel(w_ref, pos_ref, mom_ref, half_ref, far_ref, near_ref, send_ref):
    core = lax.axis_index("dom") % 2
    left = [[halves(core, block(far_ref, i, bead), block(near_ref, i, bead)) for bead in range(2)] for i in range(3)]
    right = [[halves(core, block(near_ref, i, bead), block(far_ref, i, bead)) for bead in range(2)] for i in range(3)]

    def position(plane, bead):
        if plane < 0:
            return left[plane + 2][bead]
        if plane >= OWN:
            return right[plane - OWN][bead]
        return block(pos_ref, plane, bead)

    def momentum(plane, bead):
        if plane < 0:
            return left[2][bead]
        if plane >= OWN:
            return right[2][bead]
        return block(mom_ref, plane, bead)

    def store(plane, kind, bead, value):
        half, step = place_of(plane + 1)
        send_ref[pl.ds(half * 288 + step * 4 + kind * 2 + bead, COMP, stride=12), :] = value

    for plane in range(-1, OWN + 1):
        for bead in range(2):
            store(plane, 0, bead, position(plane, bead))
    for plane in (1, 2):
        for bead in range(2):
            store(plane, 1, bead, half_ref[(plane - 1) * COMP : plane * COMP, bead * CELLS : (bead + 1) * CELLS])
    for first in (-1, OWN - 1):
        fields = [[position(first + n, bead) for bead in range(2)] for n in range(-1, 3)]
        for plane, rows in zip((first, first + 1), two_rows(w_ref, fields)):
            force = force_from(rows, jnp.concatenate([position(plane, bead) for bead in range(2)], 1))
            for bead in range(2):
                half = momentum(plane, bead) + KICK * force[:, bead * CELLS : (bead + 1) * CELLS]
                store(plane, 1, bead, half)


def bead_kernel(map_ref, in_ref, out_ref):
    columns = []
    for r in range(9):
        columns.append(jnp.concatenate([in_ref[pl.ds(r * 4 + q, GROUP, stride=36), :] for q in range(4)], 0))
    moved = jnp.dot(
        map_ref[...],
        jnp.concatenate(columns, 1),
        precision=lax.Precision.HIGHEST,
        preferred_element_type=f32,
    )
    for r in range(9):
        line, step = r // 3, r % 3
        for q in range(4):
            row = step * 2 + q if q < 2 else 6 + (step - 1) * 2 + q - 2
            if q < 2 or step > 0:
                out_ref[pl.ds(line * 10 + row, GROUP, stride=30), :] = moved[
                    q * GROUP : (q + 1) * GROUP, r * CELLS : (r + 1) * CELLS
                ]


def last_kernel(w_ref, in_ref, pos_hbm, mom_hbm, pos_ref, mom_ref, sem):
    def value(plane, kind, bead):
        half, step = place_of(plane)
        row = step * 2 + bead if kind == 0 else 6 + (step - 1) * 2 + bead
        return in_ref[pl.ds(half * 240 + row, COMP, stride=10), :]

    for plane in range(1, OWN + 1):
        for bead in range(2):
            pos_ref[pl.ds(bead * COMP * OWN + plane - 1, COMP, stride=OWN), :] = value(plane, 0, bead)
    out = pltpu.make_async_copy(pos_ref, pos_hbm, sem.at[0])
    out.start()
    for first in (1, 3):
        fields = [[value(first + n, 0, bead) for bead in range(2)] for n in range(-1, 3)]
        for plane, rows in zip((first, first + 1), two_rows(w_ref, fields)):
            force = force_from(rows, jnp.concatenate([value(plane, 0, bead) for bead in range(2)], 1))
            for bead in range(2):
                mom_ref[pl.ds(bead * COMP * OWN + plane - 1, COMP, stride=OWN), :] = (
                    value(plane, 1, bead) + KICK * force[:, bead * CELLS : (bead + 1) * CELLS]
                )
    late = pltpu.make_async_copy(mom_ref, mom_hbm, sem.at[1])
    late.start()
    out.wait()
    late.wait()


def call(kernel, name, ins, outs, scratch, flops, *args, to=VMEM):
    size = sum(int(np.prod(a.shape)) * a.dtype.itemsize for a in (*args, *outs))
    return pl.pallas_call(
        kernel,
        name=name,
        in_specs=ins,
        out_specs=[to] * len(outs),
        out_shape=list(outs),
        scratch_shapes=scratch,
        compiler_params=pltpu.CompilerParams(vmem_limit_bytes=24 * 1024 * 1024),
        cost_estimate=pl.CostEstimate(flops=flops, bytes_accessed=size, transcendentals=0),
    )(*args)


def body(positions, momenta, offsets, harmonic, cubic):
    shape = jax.ShapeDtypeStruct
    per_plane = 2 * ROWS * (QUAD * 3 // 4) * 2 * CELLS
    doms = lax.axis_size("dom")
    pos = positions.reshape(2 * COMP * OWN, CELLS)
    mom = momenta.reshape(2 * COMP * OWN, CELLS)
    own = shape((2 * COMP * OWN, CELLS), f32)
    halo = shape((6 * COMP, CELLS), f32)
    (blank,) = call(tick_kernel, "blank", [], [shape((8, CELLS), f32)], [], EARLY)
    far, near, pos, mom = call(pack_kernel, "pack", [VMEM] * 3, [halo, halo, own, own], [], EARLY, blank, pos, mom)
    between = [(i, (i + 1) % doms) for i in range(1, doms, 2)]
    far = lax.ppermute(far, "dom", between + [(j, i) for i, j in between])
    near = lax.ppermute(near, "dom", [(i, i ^ 1) for i in range(doms)])
    weights, half = call(
        inner_kernel,
        "inner",
        [SMEM] + [VMEM] * 4,
        [shape((ROWS, QUAD), bf16), shape((2 * COMP, 2 * CELLS), f32)],
        [
            pltpu.SMEM((NOFF,), jnp.int32),
            pltpu.VMEM((128, 768), f32),
            pltpu.VMEM((768, 128), f32),
        ],
        2 * per_plane,
        offsets,
        harmonic,
        cubic.T,
        pos,
        mom,
    )
    (send,) = call(
        outer_kernel, "outer", [VMEM] * 6, [shape((GROUP * 36, CELLS), f32)], [], 4 * per_plane,
        weights, pos, mom, half, far, near,
    )
    got = lax.all_to_all(send.reshape(GROUP, 9, 4, CELLS), "bead", 0, 0, tiled=True)
    (back,) = call(
        bead_kernel, "beads", [VMEM] * 2, [shape((GROUP * 30, CELLS), f32)], [], 2 * 64 * 64 * 9 * CELLS,
        jnp.asarray(propagator(GROUP)), got.reshape(GROUP * 36, CELLS),
    )
    got = lax.all_to_all(back.reshape(GROUP, 15, 2, CELLS), "bead", 0, 0, tiled=True)
    new_pos, new_mom = call(
        last_kernel, "last", [VMEM] * 2, [own] * 2,
        [pltpu.VMEM(own.shape, f32), pltpu.VMEM(own.shape, f32), pltpu.SemaphoreType.DMA((2,))],
        4 * per_plane, weights, got.reshape(GROUP * 30, CELLS), to=HBM,
    )
    return new_pos.reshape(positions.shape), new_mom.reshape(momenta.shape)


def solution(mesh):
    return jax.shard_map(
        body,
        mesh=mesh,
        in_specs=(P("bead", None, "dom", None), P("bead", None, "dom", None), P(), P(), P()),
        out_specs=(P("bead", None, "dom", None), P("bead", None, "dom", None)),
        check_vma=False,
    )
```

```python
import jax
import jax.numpy as jnp
import numpy as np
from jax import lax
from jax.experimental import pallas as pl
from jax.experimental.pallas import tpu as pltpu
from jax.sharding import PartitionSpec as P

BEADS = 32
COMP = 24
NOFF = 27
CZ = 16
CELLS = 128
OWN = 4
EXT = OWN + 2
NEAR = 9 * COMP
PART = 256
POINT = 2 * PART
QUAD = 4 * POINT
ROWS = 608
TIME_STEP = 0.5
CYCLE_FREQ = 1.0
KICK = 0.5 * TIME_STEP

EARLY = 10_000_000_000
GROUP = 16
HBM = pl.BlockSpec(memory_space=pltpu.HBM)
SMEM = pl.BlockSpec(memory_space=pltpu.SMEM)
VMEM = pl.BlockSpec(memory_space=pltpu.VMEM)
f32 = jnp.float32
bf16 = jnp.bfloat16


def propagator(groups):
    count = BEADS
    rows = np.arange(count)[:, None] * 1.0
    cols = np.arange(count)[None, :]
    angle = 2.0 * np.pi * rows * cols / count
    table = np.where(
        cols == 0,
        1.0 / np.sqrt(count) + 0.0 * angle,
        np.where(
            cols < count // 2,
            np.sqrt(2.0 / count) * np.cos(angle),
            np.where(
                cols == count // 2,
                np.cos(np.pi * rows) / np.sqrt(count),
                np.sqrt(2.0 / count) * np.sin(angle),
            ),
        ),
    )
    freq = 2.0 * CYCLE_FREQ * np.sin(np.pi * np.arange(count) / count)
    cosine = np.cos(freq * TIME_STEP)
    sine_over = np.where(
        freq > 0, np.sin(freq * TIME_STEP) / np.where(freq > 0, freq, 1.0), TIME_STEP
    )
    spring = freq * np.sin(freq * TIME_STEP)
    turn = (table * cosine) @ table.T
    drift = (table * sine_over) @ table.T
    pull = (table * spring) @ table.T
    whole = np.block([[turn, drift], [-pull, turn]])
    per = count // groups
    order = np.arange(2 * count).reshape(2, groups, per).transpose(0, 2, 1).reshape(-1)
    return whole[np.ix_(order, order)].astype(np.float32)


def bead_map():
    whole = propagator(GROUP)
    high = whole.astype(bf16)
    low = (whole - high.astype(np.float32)).astype(bf16)
    return jnp.asarray(np.concatenate([high, high, low], 1))


def neighbours(field):
    z = lax.broadcasted_iota(jnp.int32, field.shape, 1) % CZ
    up = jnp.where(z == CZ - 1, pltpu.roll(field, CZ - 1, 1), pltpu.roll(field, CELLS - 1, 1))
    down = jnp.where(z == 0, pltpu.roll(field, CELLS - CZ + 1, 1), pltpu.roll(field, 1, 1))
    along_z = [down, field, up]
    parts = [pltpu.roll(v, CZ, 1) for v in along_z]
    parts += along_z
    parts += [pltpu.roll(v, CELLS - CZ, 1) for v in along_z]
    parts.append(jnp.zeros((PART - NEAR, CELLS), f32))
    stack = jnp.concatenate(parts, 0)
    high = stack.astype(bf16)
    return (stack - high.astype(f32)).astype(bf16), high


def two_rows(w_ref, fields):
    sums = []
    for bead in range(2):
        d0, d1, d2, d3 = (plane[bead] for plane in fields)
        sums.append((d0 - d2, d1 + d2, d2 - d1, d1 - d3))
    m = []
    for q in range(4):
        low, high = (jnp.concatenate(parts, 1) for parts in zip(*(neighbours(sums[bead][q]) for bead in range(2))))
        whole = jnp.dot(w_ref[:, q * POINT : q * POINT + PART], high, preferred_element_type=f32)
        rest = jnp.dot(
            w_ref[:, q * POINT : (q + 1) * POINT], jnp.concatenate([low, high], 0), preferred_element_type=f32
        )
        m.append(whole + rest)
    return m[0] + (m[1] + m[2]), (m[1] - m[2]) - m[3]


def force_from(rows, own):
    higher = rows[: COMP * COMP].reshape(COMP, COMP, 2 * CELLS)
    anharm = jnp.sum(higher * own[None, :, :], axis=1)
    return -(rows[COMP * COMP : COMP * COMP + COMP] + anharm)


def halves(core, here, there):
    return jnp.where(core == 0, here, there)


def own_plane(ref, bead, plane):
    return ref[pl.ds(bead * COMP * OWN + plane, COMP, stride=OWN), :]


def block(ref, place, bead):
    return ref[(place * 2 + bead) * COMP : (place * 2 + bead + 1) * COMP, :]


def pair(ref, place):
    return jnp.concatenate([block(ref, place, bead) for bead in range(2)], 1)


def clear(ref, row, count):
    ref[row : row + count, :] = jnp.zeros((count, ref.shape[1]), ref.dtype)


def tick_kernel(out_ref):
    clear(out_ref, 0, 8)


def planes_kernel(ref, planes_ref):
    for plane in range(OWN):
        for bead in range(2):
            planes_ref[pl.ds((plane * 2 + bead) * COMP, COMP), :] = own_plane(ref, bead, plane)


def pack_kernel(blank_ref, raw_pos_ref, raw_mom_ref, far_ref, near_ref, pos_ref, mom_ref):
    core = lax.axis_index("dom") % 2
    planes_kernel(raw_pos_ref, pos_ref)
    planes_kernel(raw_mom_ref, mom_ref)
    for bead in range(2):
        pos = [own_plane(raw_pos_ref, bead, plane) for plane in range(OWN)]
        first, last = (own_plane(raw_mom_ref, bead, plane) for plane in (0, OWN - 1))
        for place, left, right in ((0, pos[0], pos[2]), (1, pos[1], pos[3]), (2, first, last)):
            rows = pl.ds((place * 2 + bead) * COMP, COMP)
            far_ref[rows, :] = halves(core, left, right)
            near_ref[rows, :] = halves(core, right, left)


def inner_kernel(off_ref, harm_ref, cub_ref, pos_ref, mom_ref, w_ref, half_ref, order, hpad, tail):
    fields = [[block(pos_ref, plane, bead) for bead in range(2)] for plane in range(OWN)]
    for o in range(NOFF):
        order[o] = 0
    for o in range(NOFF):
        order[off_ref[o]] = o
    clear(hpad, 0, 128)
    hpad[64 : 64 + COMP, 0 : NOFF * COMP] = harm_ref[...]
    for tile in range(6):
        tail[tile * 128 : (tile + 1) * 128, :] = hpad[:, tile * 128 : (tile + 1) * 128].T
    tail[0 : NOFF * COMP, 0:64] = cub_ref[:, 512 : COMP * COMP]

    def weights_of(code):
        rows = pl.ds(pl.multiple_of(order[code] * COMP, 8), COMP)
        return jnp.concatenate([cub_ref[rows, 0:512], tail[rows, :]], 1)

    points = [[] for _ in range(8)]
    for s in range(0, 9, 2):
        shifts = range(s, min(s + 2, 9))
        before, here, after = (
            jnp.concatenate([weights_of(dx * 9 + shift) for shift in shifts], 0) for dx in range(3)
        )
        outer = before + after
        for q, weight in enumerate((before, 0.5 * (outer + here), 0.5 * (outer - here), after)):
            if len(shifts) == 1:
                weight = jnp.concatenate([weight, jnp.zeros((PART - NEAR, 640), f32)], 0)
            high = weight.astype(bf16)
            points[2 * q].append(high)
            points[2 * q + 1].append((weight - high.astype(f32)).astype(bf16))
    for i, parts in enumerate(points):
        w_ref[:, i * PART : (i + 1) * PART] = jnp.concatenate(parts, 0).T[:ROWS]
    for plane, rows in zip((1, 2), two_rows(w_ref, fields)):
        force = force_from(rows, pair(pos_ref, plane))
        half_ref[(plane - 1) * COMP : plane * COMP, :] = pair(mom_ref, plane) + KICK * force


def place_of(plane):
    return (0, plane) if plane < 3 else (1, EXT - 1 - plane)


def outer_kernel(w_ref, pos_ref, mom_ref, half_ref, far_ref, near_ref, send_ref):
    core = lax.axis_index("dom") % 2
    left = [[halves(core, block(far_ref, i, bead), block(near_ref, i, bead)) for bead in range(2)] for i in range(3)]
    right = [[halves(core, block(near_ref, i, bead), block(far_ref, i, bead)) for bead in range(2)] for i in range(3)]

    def position(plane, bead):
        if plane < 0:
            return left[plane + 2][bead]
        if plane >= OWN:
            return right[plane - OWN][bead]
        return block(pos_ref, plane, bead)

    def momentum(plane, bead):
        if plane < 0:
            return left[2][bead]
        if plane >= OWN:
            return right[2][bead]
        return block(mom_ref, plane, bead)

    def store(plane, kind, bead, value):
        half, step = place_of(plane + 1)
        send_ref[pl.ds(half * 288 + step * 4 + kind * 2 + bead, COMP, stride=12), :] = value

    for plane in range(-1, OWN + 1):
        for bead in range(2):
            store(plane, 0, bead, position(plane, bead))
    for plane in (1, 2):
        for bead in range(2):
            store(plane, 1, bead, half_ref[(plane - 1) * COMP : plane * COMP, bead * CELLS : (bead + 1) * CELLS])
    for first in (-1, OWN - 1):
        fields = [[position(first + n, bead) for bead in range(2)] for n in range(-1, 3)]
        for plane, rows in zip((first, first + 1), two_rows(w_ref, fields)):
            force = force_from(rows, jnp.concatenate([position(plane, bead) for bead in range(2)], 1))
            for bead in range(2):
                half = momentum(plane, bead) + KICK * force[:, bead * CELLS : (bead + 1) * CELLS]
                store(plane, 1, bead, half)


def bead_kernel(map_ref, in_ref, out_ref):
    columns = []
    for r in range(9):
        columns.append(jnp.concatenate([in_ref[pl.ds(r * 4 + q, GROUP, stride=36), :] for q in range(4)], 0))
    rows = jnp.concatenate(columns, 1)
    high = rows.astype(bf16)
    low = (rows - high.astype(f32)).astype(bf16)
    moved = jnp.dot(map_ref[...], jnp.concatenate([high, low, high], 0), preferred_element_type=f32)
    for r in range(9):
        line, step = r // 3, r % 3
        for q in range(4):
            row = step * 2 + q if q < 2 else 6 + (step - 1) * 2 + q - 2
            if q < 2 or step > 0:
                out_ref[pl.ds(line * 10 + row, GROUP, stride=30), :] = moved[
                    q * GROUP : (q + 1) * GROUP, r * CELLS : (r + 1) * CELLS
                ]


def last_kernel(w_ref, in_ref, pos_hbm, mom_hbm, pos_ref, mom_ref, sem):
    def value(plane, kind, bead):
        half, step = place_of(plane)
        row = step * 2 + bead if kind == 0 else 6 + (step - 1) * 2 + bead
        return in_ref[pl.ds(half * 240 + row, COMP, stride=10), :]

    for plane in range(1, OWN + 1):
        for bead in range(2):
            pos_ref[pl.ds(bead * COMP * OWN + plane - 1, COMP, stride=OWN), :] = value(plane, 0, bead)
    out = pltpu.make_async_copy(pos_ref, pos_hbm, sem.at[0])
    out.start()
    for first in (1, 3):
        fields = [[value(first + n, 0, bead) for bead in range(2)] for n in range(-1, 3)]
        for plane, rows in zip((first, first + 1), two_rows(w_ref, fields)):
            force = force_from(rows, jnp.concatenate([value(plane, 0, bead) for bead in range(2)], 1))
            for bead in range(2):
                mom_ref[pl.ds(bead * COMP * OWN + plane - 1, COMP, stride=OWN), :] = (
                    value(plane, 1, bead) + KICK * force[:, bead * CELLS : (bead + 1) * CELLS]
                )
    late = pltpu.make_async_copy(mom_ref, mom_hbm, sem.at[1])
    late.start()
    out.wait()
    late.wait()


def call(kernel, name, ins, outs, scratch, flops, *args, to=VMEM):
    size = sum(int(np.prod(a.shape)) * a.dtype.itemsize for a in (*args, *outs))
    return pl.pallas_call(
        kernel,
        name=name,
        in_specs=ins,
        out_specs=[to] * len(outs),
        out_shape=list(outs),
        scratch_shapes=scratch,
        compiler_params=pltpu.CompilerParams(vmem_limit_bytes=24 * 1024 * 1024),
        cost_estimate=pl.CostEstimate(flops=flops, bytes_accessed=size, transcendentals=0),
    )(*args)


def body(positions, momenta, offsets, harmonic, cubic):
    shape = jax.ShapeDtypeStruct
    per_plane = 2 * ROWS * (QUAD * 3 // 4) * 2 * CELLS
    doms = lax.axis_size("dom")
    pos = positions.reshape(2 * COMP * OWN, CELLS)
    mom = momenta.reshape(2 * COMP * OWN, CELLS)
    own = shape((2 * COMP * OWN, CELLS), f32)
    halo = shape((6 * COMP, CELLS), f32)
    (blank,) = call(tick_kernel, "blank", [], [shape((8, CELLS), f32)], [], EARLY)
    far, near, pos, mom = call(pack_kernel, "pack", [VMEM] * 3, [halo, halo, own, own], [], EARLY, blank, pos, mom)
    between = [(i, (i + 1) % doms) for i in range(1, doms, 2)]
    far = lax.ppermute(far, "dom", between + [(j, i) for i, j in between])
    near = lax.ppermute(near, "dom", [(i, i ^ 1) for i in range(doms)])
    weights, half = call(
        inner_kernel,
        "inner",
        [SMEM] + [VMEM] * 4,
        [shape((ROWS, QUAD), bf16), shape((2 * COMP, 2 * CELLS), f32)],
        [
            pltpu.SMEM((NOFF,), jnp.int32),
            pltpu.VMEM((128, 768), f32),
            pltpu.VMEM((768, 128), f32),
        ],
        2 * per_plane,
        offsets,
        harmonic,
        cubic.T,
        pos,
        mom,
    )
    (send,) = call(
        outer_kernel, "outer", [VMEM] * 6, [shape((GROUP * 36, CELLS), f32)], [], 4 * per_plane,
        weights, pos, mom, half, far, near,
    )
    got = lax.all_to_all(send.reshape(GROUP, 9, 4, CELLS), "bead", 0, 0, tiled=True)
    (back,) = call(
        bead_kernel, "beads", [VMEM] * 2, [shape((GROUP * 30, CELLS), f32)], [], 2 * 64 * 64 * 9 * CELLS,
        bead_map(), got.reshape(GROUP * 36, CELLS),
    )
    got = lax.all_to_all(back.reshape(GROUP, 15, 2, CELLS), "bead", 0, 0, tiled=True)
    new_pos, new_mom = call(
        last_kernel, "last", [VMEM] * 2, [own] * 2,
        [pltpu.VMEM(own.shape, f32), pltpu.VMEM(own.shape, f32), pltpu.SemaphoreType.DMA((2,))],
        4 * per_plane, weights, got.reshape(GROUP * 30, CELLS), to=HBM,
    )
    return new_pos.reshape(positions.shape), new_mom.reshape(momenta.shape)


def solution(mesh):
    return jax.shard_map(
        body,
        mesh=mesh,
        in_specs=(P("bead", None, "dom", None), P("bead", None, "dom", None), P(), P(), P()),
        out_specs=(P("bead", None, "dom", None), P("bead", None, "dom", None)),
        check_vma=False,
    )
```

```python
import jax
import jax.numpy as jnp
import numpy as np
from jax import lax
from jax.experimental import pallas as pl
from jax.experimental.pallas import tpu as pltpu
from jax.sharding import PartitionSpec as P

BEADS = 32
COMP = 24
NOFF = 27
CZ = 16
CELLS = 128
OWN = 4
EXT = OWN + 2
NEAR = 9 * COMP
PART = 256
POINT = 2 * PART
QUAD = 4 * POINT
ROWS = 608
TIME_STEP = 0.5
CYCLE_FREQ = 1.0
KICK = 0.5 * TIME_STEP

EARLY = 10_000_000_000
GROUP = 16
HBM = pl.BlockSpec(memory_space=pltpu.HBM)
SMEM = pl.BlockSpec(memory_space=pltpu.SMEM)
VMEM = pl.BlockSpec(memory_space=pltpu.VMEM)
f32 = jnp.float32
bf16 = jnp.bfloat16


def propagator(groups):
    count = BEADS
    rows = np.arange(count)[:, None] * 1.0
    cols = np.arange(count)[None, :]
    angle = 2.0 * np.pi * rows * cols / count
    table = np.where(
        cols == 0,
        1.0 / np.sqrt(count) + 0.0 * angle,
        np.where(
            cols < count // 2,
            np.sqrt(2.0 / count) * np.cos(angle),
            np.where(
                cols == count // 2,
                np.cos(np.pi * rows) / np.sqrt(count),
                np.sqrt(2.0 / count) * np.sin(angle),
            ),
        ),
    )
    freq = 2.0 * CYCLE_FREQ * np.sin(np.pi * np.arange(count) / count)
    cosine = np.cos(freq * TIME_STEP)
    sine_over = np.where(
        freq > 0, np.sin(freq * TIME_STEP) / np.where(freq > 0, freq, 1.0), TIME_STEP
    )
    spring = freq * np.sin(freq * TIME_STEP)
    turn = (table * cosine) @ table.T
    drift = (table * sine_over) @ table.T
    pull = (table * spring) @ table.T
    whole = np.block([[turn, drift], [-pull, turn]])
    per = count // groups
    order = np.arange(2 * count).reshape(2, groups, per).transpose(0, 2, 1).reshape(-1)
    return whole[np.ix_(order, order)].astype(np.float32)


def bead_map():
    whole = propagator(GROUP)
    high = whole.astype(bf16)
    low = (whole - high.astype(np.float32)).astype(bf16)
    return jnp.asarray(np.concatenate([high, high, low], 1))


def neighbours(field):
    z = lax.broadcasted_iota(jnp.int32, field.shape, 1) % CZ
    up = jnp.where(z == CZ - 1, pltpu.roll(field, CZ - 1, 1), pltpu.roll(field, CELLS - 1, 1))
    down = jnp.where(z == 0, pltpu.roll(field, CELLS - CZ + 1, 1), pltpu.roll(field, 1, 1))
    along_z = [down, field, up]
    parts = [pltpu.roll(v, CZ, 1) for v in along_z]
    parts += along_z
    parts += [pltpu.roll(v, CELLS - CZ, 1) for v in along_z]
    parts.append(jnp.zeros((PART - NEAR, CELLS), f32))
    stack = jnp.concatenate(parts, 0)
    high = stack.astype(bf16)
    return (stack - high.astype(f32)).astype(bf16), high


def two_rows(w_ref, fields):
    sums = []
    for bead in range(2):
        d0, d1, d2, d3 = (plane[bead] for plane in fields)
        sums.append((d0 - d2, d1 + d2, d2 - d1, d1 - d3))
    m = []
    for q in range(4):
        low, high = (jnp.concatenate(parts, 1) for parts in zip(*(neighbours(sums[bead][q]) for bead in range(2))))
        whole = jnp.dot(w_ref[:, q * POINT : q * POINT + PART], high, preferred_element_type=f32)
        rest = jnp.dot(
            w_ref[:, q * POINT : (q + 1) * POINT], jnp.concatenate([low, high], 0), preferred_element_type=f32
        )
        m.append(whole + rest)
    return m[0] + (m[1] + m[2]), (m[1] - m[2]) - m[3]


def force_from(rows, own):
    higher = rows[: COMP * COMP].reshape(COMP, COMP, 2 * CELLS)
    anharm = jnp.sum(higher * own[None, :, :], axis=1)
    return -(rows[COMP * COMP : COMP * COMP + COMP] + anharm)


def halves(core, here, there):
    return jnp.where(core == 0, here, there)


def own_plane(ref, bead, plane):
    return ref[pl.ds(bead * COMP * OWN + plane, COMP, stride=OWN), :]


def block(ref, place, bead):
    return ref[(place * 2 + bead) * COMP : (place * 2 + bead + 1) * COMP, :]


def pair(ref, place):
    return jnp.concatenate([block(ref, place, bead) for bead in range(2)], 1)


def clear(ref, row, count):
    ref[row : row + count, :] = jnp.zeros((count, ref.shape[1]), ref.dtype)


def tick_kernel(out_ref):
    clear(out_ref, 0, 8)


def planes_kernel(ref, planes_ref):
    for plane in range(OWN):
        for bead in range(2):
            planes_ref[pl.ds((plane * 2 + bead) * COMP, COMP), :] = own_plane(ref, bead, plane)


def pack_kernel(blank_ref, raw_pos_ref, raw_mom_ref, far_ref, near_ref, pos_ref, mom_ref):
    core = lax.axis_index("dom") % 2
    planes_kernel(raw_pos_ref, pos_ref)
    planes_kernel(raw_mom_ref, mom_ref)
    for bead in range(2):
        pos = [own_plane(raw_pos_ref, bead, plane) for plane in range(OWN)]
        first, last = (own_plane(raw_mom_ref, bead, plane) for plane in (0, OWN - 1))
        for place, left, right in ((0, pos[0], pos[2]), (1, pos[1], pos[3]), (2, first, last)):
            rows = pl.ds((place * 2 + bead) * COMP, COMP)
            far_ref[rows, :] = halves(core, left, right)
            near_ref[rows, :] = halves(core, right, left)


def inner_kernel(off_ref, harm_ref, cub_ref, pos_ref, mom_ref, w_ref, half_ref, order, hpad, tail):
    fields = [[block(pos_ref, plane, bead) for bead in range(2)] for plane in range(OWN)]
    for o in range(NOFF):
        order[o] = 0
    for o in range(NOFF):
        order[off_ref[o]] = o
    clear(hpad, 0, 128)
    hpad[64 : 64 + COMP, 0 : NOFF * COMP] = harm_ref[...]
    for tile in range(6):
        tail[tile * 128 : (tile + 1) * 128, :] = hpad[:, tile * 128 : (tile + 1) * 128].T
    tail[0 : NOFF * COMP, 0:64] = cub_ref[:, 512 : COMP * COMP]

    def weights_of(code):
        rows = pl.ds(pl.multiple_of(order[code] * COMP, 8), COMP)
        return jnp.concatenate([cub_ref[rows, 0:512], tail[rows, :]], 1)

    points = [[] for _ in range(8)]
    for s in range(0, 9, 2):
        shifts = range(s, min(s + 2, 9))
        before, here, after = (
            jnp.concatenate([weights_of(dx * 9 + shift) for shift in shifts], 0) for dx in range(3)
        )
        outer = before + after
        for q, weight in enumerate((before, 0.5 * (outer + here), 0.5 * (outer - here), after)):
            if len(shifts) == 1:
                weight = jnp.concatenate([weight, jnp.zeros((PART - NEAR, 640), f32)], 0)
            high = weight.astype(bf16)
            points[2 * q].append(high)
            points[2 * q + 1].append((weight - high.astype(f32)).astype(bf16))
    for i, parts in enumerate(points):
        w_ref[:, i * PART : (i + 1) * PART] = jnp.concatenate(parts, 0).T[:ROWS]
    for plane, rows in zip((1, 2), two_rows(w_ref, fields)):
        force = force_from(rows, pair(pos_ref, plane))
        half_ref[(plane - 1) * COMP : plane * COMP, :] = pair(mom_ref, plane) + KICK * force


def place_of(plane):
    return (0, plane) if plane < 3 else (1, EXT - 1 - plane)


def outer_kernel(w_ref, pos_ref, mom_ref, half_ref, far_ref, near_ref, send_ref):
    core = lax.axis_index("dom") % 2
    left = [[halves(core, block(far_ref, i, bead), block(near_ref, i, bead)) for bead in range(2)] for i in range(3)]
    right = [[halves(core, block(near_ref, i + 3, bead), block(far_ref, i, bead)) for bead in range(2)] for i in range(3)]

    def position(plane, bead):
        if plane < 0:
            return left[plane + 2][bead]
        if plane >= OWN:
            return right[plane - OWN][bead]
        return block(pos_ref, plane, bead)

    def momentum(plane, bead):
        if plane < 0:
            return left[2][bead]
        if plane >= OWN:
            return right[2][bead]
        return block(mom_ref, plane, bead)

    def store(plane, kind, bead, value):
        half, step = place_of(plane + 1)
        send_ref[pl.ds(half * 288 + step * 4 + kind * 2 + bead, COMP, stride=12), :] = value

    for plane in range(-1, OWN + 1):
        for bead in range(2):
            store(plane, 0, bead, position(plane, bead))
    for plane in (1, 2):
        for bead in range(2):
            store(plane, 1, bead, half_ref[(plane - 1) * COMP : plane * COMP, bead * CELLS : (bead + 1) * CELLS])
    for first in (-1, OWN - 1):
        fields = [[position(first + n, bead) for bead in range(2)] for n in range(-1, 3)]
        for plane, rows in zip((first, first + 1), two_rows(w_ref, fields)):
            force = force_from(rows, jnp.concatenate([position(plane, bead) for bead in range(2)], 1))
            for bead in range(2):
                half = momentum(plane, bead) + KICK * force[:, bead * CELLS : (bead + 1) * CELLS]
                store(plane, 1, bead, half)


def bead_kernel(map_ref, in_ref, out_ref):
    columns = []
    for r in range(9):
        columns.append(jnp.concatenate([in_ref[pl.ds(r * 4 + q, GROUP, stride=36), :] for q in range(4)], 0))
    rows = jnp.concatenate(columns, 1)
    high = rows.astype(bf16)
    low = (rows - high.astype(f32)).astype(bf16)
    moved = jnp.dot(map_ref[...], jnp.concatenate([high, low, high], 0), preferred_element_type=f32)
    for r in range(9):
        line, step = r // 3, r % 3
        for q in range(4):
            row = step * 2 + q if q < 2 else 6 + (step - 1) * 2 + q - 2
            if q < 2 or step > 0:
                out_ref[pl.ds(line * 10 + row, GROUP, stride=30), :] = moved[
                    q * GROUP : (q + 1) * GROUP, r * CELLS : (r + 1) * CELLS
                ]


def last_kernel(w_ref, in_ref, pos_hbm, mom_hbm, pos_ref, mom_ref, sem):
    def value(plane, kind, bead):
        half, step = place_of(plane)
        row = step * 2 + bead if kind == 0 else 6 + (step - 1) * 2 + bead
        return in_ref[pl.ds(half * 240 + row, COMP, stride=10), :]

    for plane in range(1, OWN + 1):
        for bead in range(2):
            pos_ref[pl.ds(bead * COMP * OWN + plane - 1, COMP, stride=OWN), :] = value(plane, 0, bead)
    out = pltpu.make_async_copy(pos_ref, pos_hbm, sem.at[0])
    out.start()
    for first in (1, 3):
        fields = [[value(first + n, 0, bead) for bead in range(2)] for n in range(-1, 3)]
        for plane, rows in zip((first, first + 1), two_rows(w_ref, fields)):
            force = force_from(rows, jnp.concatenate([value(plane, 0, bead) for bead in range(2)], 1))
            for bead in range(2):
                mom_ref[pl.ds(bead * COMP * OWN + plane - 1, COMP, stride=OWN), :] = (
                    value(plane, 1, bead) + KICK * force[:, bead * CELLS : (bead + 1) * CELLS]
                )
    late = pltpu.make_async_copy(mom_ref, mom_hbm, sem.at[1])
    late.start()
    out.wait()
    late.wait()


def call(kernel, name, ins, outs, scratch, flops, *args, to=VMEM):
    size = sum(int(np.prod(a.shape)) * a.dtype.itemsize for a in (*args, *outs))
    return pl.pallas_call(
        kernel,
        name=name,
        in_specs=ins,
        out_specs=[to] * len(outs),
        out_shape=list(outs),
        scratch_shapes=scratch,
        compiler_params=pltpu.CompilerParams(vmem_limit_bytes=24 * 1024 * 1024),
        cost_estimate=pl.CostEstimate(flops=flops, bytes_accessed=size, transcendentals=0),
    )(*args)


def body(positions, momenta, offsets, harmonic, cubic):
    shape = jax.ShapeDtypeStruct
    per_plane = 2 * ROWS * (QUAD * 3 // 4) * 2 * CELLS
    doms = lax.axis_size("dom")
    pos = positions.reshape(2 * COMP * OWN, CELLS)
    mom = momenta.reshape(2 * COMP * OWN, CELLS)
    own = shape((2 * COMP * OWN, CELLS), f32)
    halo = shape((6 * COMP, CELLS), f32)
    (blank,) = call(tick_kernel, "blank", [], [shape((8, CELLS), f32)], [], EARLY)
    far, near, pos, mom = call(pack_kernel, "pack", [VMEM] * 3, [halo, halo, own, own], [], EARLY, blank, pos, mom)
    between = [(i, (i + 1) % doms) for i in range(1, doms, 2)]
    far = lax.ppermute(far, "dom", between + [(j, i) for i, j in between])
    near = lax.all_gather(near, "dom", axis_index_groups=[[i, i + 1] for i in range(0, doms, 2)], tiled=True)
    weights, half = call(
        inner_kernel,
        "inner",
        [SMEM] + [VMEM] * 4,
        [shape((ROWS, QUAD), bf16), shape((2 * COMP, 2 * CELLS), f32)],
        [
            pltpu.SMEM((NOFF,), jnp.int32),
            pltpu.VMEM((128, 768), f32),
            pltpu.VMEM((768, 128), f32),
        ],
        2 * per_plane,
        offsets,
        harmonic,
        cubic.T,
        pos,
        mom,
    )
    (send,) = call(
        outer_kernel, "outer", [VMEM] * 6, [shape((GROUP * 36, CELLS), f32)], [], 4 * per_plane,
        weights, pos, mom, half, far, near,
    )
    got = lax.all_to_all(send.reshape(GROUP, 9, 4, CELLS), "bead", 0, 0, tiled=True)
    (back,) = call(
        bead_kernel, "beads", [VMEM] * 2, [shape((GROUP * 30, CELLS), f32)], [], 2 * 64 * 64 * 9 * CELLS,
        bead_map(), got.reshape(GROUP * 36, CELLS),
    )
    got = lax.all_to_all(back.reshape(GROUP, 15, 2, CELLS), "bead", 0, 0, tiled=True)
    new_pos, new_mom = call(
        last_kernel, "last", [VMEM] * 2, [own] * 2,
        [pltpu.VMEM(own.shape, f32), pltpu.VMEM(own.shape, f32), pltpu.SemaphoreType.DMA((2,))],
        4 * per_plane, weights, got.reshape(GROUP * 30, CELLS), to=HBM,
    )
    return new_pos.reshape(positions.shape), new_mom.reshape(momenta.shape)


def solution(mesh):
    return jax.shard_map(
        body,
        mesh=mesh,
        in_specs=(P("bead", None, "dom", None), P("bead", None, "dom", None), P(), P(), P()),
        out_specs=(P("bead", None, "dom", None), P("bead", None, "dom", None)),
        check_vma=False,
    )
```
